256 devices in a mesh: group: 16 (over x, y), hash: 16 (over z, core).
Axes of the slice: x: 4, y: 4, z: 8, core: 2. Of those that a mesh axis runs over, the one named last changes fastest.
Arguments:
- pooled: bfloat16 [16, 2048, 32, 256], P('hash', 'group'), may hold values from -0.375 to 0.375
- weight: bfloat16 [1024, 2048], replicated, may hold values from -0.1875 to 0.1875
- cotangent: bfloat16 [16, 2048, 2048], P('hash', 'group'), may hold values from -6 to 6
- owners: int32 [16, 32, 2048, 2], P('hash', 'group'), may hold values from 0 to 15, all different within a row; in each aligned block of 4096 rows (0 to 4095, 4096 to 8191, ..., all dimensions but the last counted through in order) at most 682 rows name the same one
- local_rows: int32 [16, 32, 2048, 2], P('hash', 'group'), may hold values from 0 to 511
- table: float32 [32, 8192, 256], P('group', 'hash'), may hold values from -0.625 to 0.625
- accum: float32 [32, 8192], P('group', 'hash'), may hold values from 0.05 to 2
Outputs:
- wgrad: bfloat16 [1024, 2048], replicated
- table_out: float32 [32, 8192, 256], P('group', 'hash')
- accum_out: float32 [32, 8192], P('group', 'hash')
The draws below stay inside these ranges and needn't reach their ends.
Inputs may be any that keep to these rules, and one draw needn't show every extreme that they name: Among the rows of one device (aligned blocks of 4096 bags), no owner is named more than 682 times, a bound that some block reaches; the 2 owners of one bag differ.
All inputs are finite; a program needn't handle non-finite values.
Results may differ from the reference program's by a relative error of at most 0.0059.
Values may be sent and summed in bfloat16 or wider, within the bound.
A program may use at most 128 MiB of HBM per device.

```python
import math
import jax
import jax.numpy as jnp
import numpy as np
from jax import lax

E = 256
H = 2048
FEATS = 32
L = 2
S_DEV = 128
ROWS_DEV = 512
PAIRS = 1024
SAMPLES = 32768
CAP = 682
N_GROUP = 16
N_HASH = 16


def with_ends(array, key, least, largest):
    place = [jax.random.randint(jax.random.fold_in(key, axis), (), 0, length) for axis, length in enumerate(array.shape)]
    main_axis = array.shape.index(max(array.shape))
    neighbour = place[:main_axis] + [(place[main_axis] + 1) % array.shape[main_axis]] + place[main_axis + 1:]
    return array.at[tuple(place)].set(least).at[tuple(neighbour)].set(largest)


def levels(own_key, extent, pieces, low, top_value):
    def one(axis_at, shards_of):
        steps = jax.random.uniform(jax.random.fold_in(jax.random.fold_in(own_key, 6), axis_at), (shards_of,), jnp.float32, low / len(pieces), top_value / len(pieces))
        return jnp.repeat(jnp.exp(steps), extent[axis_at] // shards_of).reshape((-1,) + (1,) * (len(extent) - axis_at - 1))

    loudness = one(*pieces[0])
    for cut in pieces[1:]:
        loudness = loudness * one(*cut)
    return loudness


def cumulative_ranks(number_of, slope):
    loads = [(1 << 20) // math.isqrt(rank ** slope) + 1 for rank in range(1, number_of + 1)]
    width = 1 + sum(loads) // (1 << 30)
    return np.cumsum(np.array([max(1, weight // width) for weight in loads]))


def skewed_ids(stream_key, shape, amount, skew):
    listing = cumulative_ranks(amount, skew)
    pick = jax.random.randint(jax.random.fold_in(stream_key, 1), shape, 0, int(listing[amount - 1]))
    rank = jnp.searchsorted(jnp.asarray(listing, jnp.int32), pick, side="right")
    return jax.random.permutation(jax.random.fold_in(stream_key, 2), amount)[rank].astype(jnp.int32)


def shared_out(own_key, own, number, rows, count, top, most, lean):
    order = jax.random.permutation(own_key, count)
    heavy_load, ordinary = portions_of(count, rows * top, most, lean, True), portions_of(count, rows * top, most, lean, False)
    places = jnp.arange(count)

    def named(tallies, rotation):
        used = int((tallies > 0).sum())
        fixed = max(1, used // 4)
        shifted = fixed + (places - fixed + rotation * (used - fixed)) % max(1, count - fixed)
        return jnp.zeros((count,), jnp.int32).at[order[jnp.where(places < fixed, places, shifted)]].set(jnp.asarray(tallies, jnp.int32))

    tallies = jnp.where(number % 4 == 0, named(heavy_load, number // 4), named(ordinary, number - number // 4 - 1))
    mixed = jax.random.permutation(jax.random.fold_in(own, 3), count)
    giver, sink = mixed[0:count // 2 * 2:2], mixed[1:count // 2 * 2:2]
    margin = jnp.minimum(tallies[giver] - 1, most - tallies[sink]) // 2
    margin = jnp.where((giver == order[0]) | (sink == order[0]) | (tallies[sink] == 0), 0, jnp.maximum(margin, 0))
    shifted = jax.random.randint(jax.random.fold_in(own, 4), (count // 2,), 0, 1 << 20) % (margin + 1)
    tallies = tallies.at[giver].add(-shifted).at[sink].add(shifted)
    items = jnp.searchsorted(jnp.cumsum(tallies), jnp.arange(rows * top), side="right").astype(jnp.int32)
    listing = items.reshape(top, rows).T
    listing = listing[jax.random.permutation(jax.random.fold_in(own, 1), rows)]
    rotation = jax.random.randint(jax.random.fold_in(own, 2), (rows, 1), 0, top)
    return jnp.take_along_axis(listing, (jnp.arange(top)[None, :] + rotation) % top, axis=1)


def portions_of(count, total, reach, lean, full):
    loads = [(1 << 20) // math.isqrt(standing ** lean) + 1 for standing in range(1, count + 1)]
    largest = reach if full else min(reach, max(-(-total // count), total * loads[0] // sum(loads)))
    least = 1 if total - largest >= count - 1 else 0
    counts, surplus = [largest] + [least] * (count - 1), total - largest - least * (count - 1)
    while surplus > 0:
        movable = [i for i in range(1, count) if counts[i] < largest] or [i for i in range(1, count) if counts[i] < reach]
        whole, budget = sum([loads[i] for i in movable]), surplus
        for i in movable:
            extra = min(reach - counts[i], max(1, budget * loads[i] // whole), surplus)
            counts[i] = counts[i] + extra
            surplus = surplus - extra
    return np.array(counts)


def bell_draw(own_key, dims, spread, limit, pieces=(), kind=jnp.bfloat16):
    array = jax.random.normal(own_key, dims, jnp.float32) * spread
    if len(pieces) > 0:
        array = levels(own_key, dims, pieces, -0.22, 0.18) * array
    return jnp.clip(array, min=-limit, max=limit).astype(kind)


def setup_inputs(seed: int = 0) -> dict:
    key_list = jax.random.split(jax.random.key(seed), 8)
    pooled = bell_draw(key_list[0], (N_HASH, N_GROUP * S_DEV, FEATS, E), 0.0625, 0.375, ((0, 16), (1, 16)))
    weight = bell_draw(key_list[1], (PAIRS, H), PAIRS ** -0.5, 0.1875)
    cotangent = bell_draw(key_list[2], (N_HASH, N_GROUP * S_DEV, H), 1.0, 6.0, ((0, 16), (1, 16)))
    owners_keys = jax.random.split(jax.random.fold_in(key_list[3], 1), N_HASH * FEATS * (N_GROUP * S_DEV) // (FEATS * S_DEV))
    owners_turns = jax.random.permutation(jax.random.fold_in(key_list[3], 3), N_HASH * FEATS * (N_GROUP * S_DEV) // (FEATS * S_DEV))
    owners = jax.vmap(lambda own, number: shared_out(jax.random.fold_in(key_list[3], 2), own, number, FEATS * S_DEV, N_HASH, L, CAP, 1))(owners_keys, owners_turns).reshape((N_HASH, FEATS, N_GROUP * S_DEV, L))
    local_rows = with_ends(skewed_ids(key_list[4], (N_HASH, FEATS, N_GROUP * S_DEV, L), ROWS_DEV, 2), jax.random.fold_in(key_list[4], 3), 0, ROWS_DEV - 1).astype(jnp.int32)
    table = bell_draw(key_list[5], (FEATS, N_HASH * ROWS_DEV, E), 0.1, 0.625, ((0, 16), (1, 16)), jnp.float32)
    accum = jnp.clip(jnp.exp(math.log(2.0) - 3.6888794 * jax.random.uniform(key_list[6], (FEATS, N_HASH * ROWS_DEV), jnp.float32) ** levels(key_list[6], (FEATS, N_HASH * ROWS_DEV), ((0, 16), (1, 16)), -0.2, 0.2)), 0.05, 2.0)
    return dict(pooled=pooled, weight=weight, cotangent=cotangent, owners=owners, local_rows=local_rows, table=table, accum=accum)


def reference(pooled, weight, cotangent, owners, local_rows, table, accum):

    def step(carry, inputs):
        wsum, rsum = carry
        vectors, cotan, owner_block, row_block = inputs
        count = vectors.shape[0]
        inter = jnp.einsum('sfe,sge->sfg', vectors.astype(jnp.float32), vectors.astype(jnp.float32)).astype(jnp.bfloat16)
        inter_rows = inter.reshape(count, FEATS * FEATS)
        preact = jnp.dot(inter_rows, weight, preferred_element_type=jnp.float32)
        sigmoid_v = jax.nn.sigmoid(preact)
        dpre = (cotan.astype(jnp.float32) * (sigmoid_v * (1.0 + preact * (1.0 - sigmoid_v)))).astype(jnp.bfloat16)
        wsum = wsum + lax.dot_general(inter_rows, dpre, (((0,), (0,)), ((), ())), preferred_element_type=jnp.float32)
        dinter = lax.dot_general(dpre, weight, (((1,), (1,)), ((), ())), preferred_element_type=jnp.float32).reshape(count, FEATS, FEATS)
        dsym = (dinter + jnp.swapaxes(dinter, 1, 2)).astype(jnp.bfloat16)
        dpooled = jnp.einsum('sfg,sge->fse', dsym.astype(jnp.float32), vectors.astype(jnp.float32)).astype(jnp.bfloat16)
        keys = (owner_block * ROWS_DEV + row_block).astype(jnp.int32)
        values = jnp.broadcast_to(dpooled[:, :, None, :].astype(jnp.float32), keys.shape + (E,))

        def one_feature(vals, feature_keys):
            return jax.ops.segment_sum(vals.reshape(-1, E), feature_keys.reshape(-1), num_segments=N_HASH * ROWS_DEV)
        rsum = rsum + jax.vmap(one_feature)(values, keys)
        return ((wsum, rsum), None)
    start = (jnp.zeros((FEATS * FEATS, H), jnp.float32), jnp.zeros((FEATS, N_HASH * ROWS_DEV, E), jnp.float32))
    (wsum, rowgrad), _ = lax.scan(step, start, (pooled, cotangent, owners, local_rows))
    wgrad = (wsum / math.sqrt(SAMPLES)).astype(jnp.bfloat16)
    accum_out = accum + lax.optimization_barrier(jnp.mean(rowgrad * rowgrad, axis=-1))
    table_out = table - 0.1 * rowgrad / jnp.sqrt(accum_out)[:, :, None]
    return (wgrad, table_out, accum_out)
```

```python
import math

import jax
import jax.numpy as jnp
from jax import lax
from jax.experimental import pallas as pl
from jax.experimental.pallas import tpu as pltpu
from jax.sharding import Mesh, PartitionSpec as P

AXES = ("x", "y", "z", "core")
BF = jnp.bfloat16
F32 = jnp.float32


def make_kernel(nx, ny, nz, samples, width, rows, scale):
    far = nz // 2
    half_s = samples // 2
    half_r = rows // 2

    def kernel(
        dp, inter, dpre, keys, g_out, row_out,
        a1, b1, v, kbuf, sb, rb, sw, rw, w, r1, t, r2, u, r3, gz, g,
        ks, s1s, s1r, s2s, s2r, loc, vs, zs, zr, ws, x1s, x1r, x2s, x2r, x3s, x3r,
        g0s, g0r, g1s, g1r, g2s, g2r, hs, hr, os,
    ):
        x, y, z, c = (lax.axis_index(a) for a in AXES)
        here = {"x": (x, nx), "y": (y, ny), "z": (z, nz), "core": (c, 2)}
        other = 1 - c
        pending = []

        def device(axis, d):
            me, n = here[axis]
            place = {a: here[a][0] for a in AXES}
            place[axis] = lax.rem(me + d + n, n)
            return tuple(place[a] for a in AXES)

        def peer(axis, d):
            me, n = here[axis]
            return lax.rem(me + d + n, n)

        def send(src, dst, ssem, rsem, axis, d):
            copy = pltpu.make_async_remote_copy(
                src, dst, ssem, rsem, device_id=device(axis, d), device_id_type=pl.DeviceIdType.MESH
            )
            copy.start()
            pending.append(copy)
            return copy

        def local_copy(src, dst, sem):
            copy = pltpu.make_async_copy(src, dst, sem)
            copy.start()
            return copy

        barrier = pltpu.get_barrier_semaphore()
        greeted = 0
        for axis, n in (("core", 2), ("x", nx), ("y", ny), ("z", nz)):
            for d in range(1, n):
                pl.semaphore_signal(
                    barrier, inc=1, device_id=device(axis, d), device_id_type=pl.DeviceIdType.MESH
                )
                greeted += 1
        pl.semaphore_wait(barrier, greeted)

        def first_hop(j):
            copies = []
            for d in range(1, max(nx, ny)):
                if d < nx:
                    copies.append(send(
                        dp.at[peer("x", d), :, j, pl.ds(0, half_s), :], a1.at[j, x],
                        s1s.at[j, 0, d - 1], s1r.at[j, 0, d - 1], "x", d,
                    ))
                if d < ny:
                    copies.append(send(
                        dp.at[:, peer("y", d), j, pl.ds(half_s, half_s), :], b1.at[j, y],
                        s1s.at[j, 1, d - 1], s1r.at[j, 1, d - 1], "y", d,
                    ))
            own = [
                local_copy(dp.at[x, :, j, pl.ds(0, half_s), :], a1.at[j, x], loc.at[j, 0]),
                local_copy(dp.at[:, y, j, pl.ds(half_s, half_s), :], b1.at[j, y], loc.at[j, 1]),
            ]
            return copies, own

        def arrived(copies, own=()):
            for copy in own:
                copy.wait()
            for copy in copies:
                copy.wait_recv()

        def second_hop(j):
            copies = []
            for d in range(1, max(nx, ny)):
                if d < ny:
                    copies.append(send(
                        a1.at[j, :, peer("y", d)], v.at[j, c, :, y, pl.ds(0, half_s), :],
                        s2s.at[j, 0, d - 1], s2r.at[j, 0, d - 1], "y", d,
                    ))
                if d < nx:
                    copies.append(send(
                        b1.at[j, :, peer("x", d)], v.at[j, c, x, :, pl.ds(half_s, half_s), :],
                        s2s.at[j, 1, d - 1], s2r.at[j, 1, d - 1], "x", d,
                    ))
            own = [
                local_copy(a1.at[j, :, y], v.at[j, c, :, y, pl.ds(0, half_s), :], loc.at[j, 2]),
                local_copy(b1.at[j, :, x], v.at[j, c, x, :, pl.ds(half_s, half_s), :], loc.at[j, 3]),
            ]
            return copies, own

        def share_values(j):
            return send(v.at[j, c], v.at[j, c], vs.at[j, 0], vs.at[j, 1], "core", 1)

        def term(core, ab, m, n_minor):
            r = w.shape[3]
            cols = n_minor * 128
            return lax.dot_general(
                inter[:, pl.ds(pl.multiple_of((core * 2 + ab) * r, 128), r)],
                dpre[:, m * cols : (m + 1) * cols],
                (((0,), (0,)), ((), ())),
                preferred_element_type=F32,
            )

        minors = (ny, nx)
        majors = (nx, ny)

        def partial(j, dest, half):
            base = (2 * dest + c) * rows + half * half_r
            iota = lax.broadcasted_iota(jnp.int32, (half_r, ny * samples), 0).astype(jnp.int16)

            def chunk(q, acc):
                h = lax.rem(c + q // nx, 2)
                i = lax.rem(q, nx)
                first = (kbuf[h, i, 2 * j : 2 * j + 1, :] - base).astype(jnp.int16)
                second = (kbuf[h, i, 2 * j + 1 : 2 * j + 2, :] - base).astype(jnp.int16)
                hot = jnp.where((iota == first) | (iota == second), BF(1), BF(0))
                return acc + jnp.dot(
                    hot, v[j, h, i].reshape(ny * samples, width), preferred_element_type=F32
                )

            return lax.fori_loop(0, 2 * nx, chunk, jnp.zeros((half_r, width), F32))

        def part(half):
            return pl.ds(half * half_r, half_r)

        ring = {}

        def comes(k, way, half):
            return k < far or (k == far and way == half)

        def ring_item(j, k, way, half):
            total = partial(j, peer("z", k if way == 0 else -k), half)
            if comes(k + 1, way, half):
                ring[j, k + 1, way, half].wait_recv()
                total = total + rb[j, way, k, part(half), :].astype(F32)
            sb[j, way, k - 1, part(half), :] = total.astype(BF)
            ring[j, k, way, half] = send(
                sb.at[j, way, k - 1, part(half), :], rb.at[j, way, k - 1, part(half), :],
                zs.at[j, way, k - 1, half], zr.at[j, way, k - 1, half], "z", 1 if way == 0 else -1,
            )

        def ring_items(j):
            items = []
            for k in range(far, 0, -1):
                for way, half in ((0, 0), (1, 1), (0, 1), (1, 0)):
                    if comes(k, way, half):
                        items.append((j, k, way, half))
            return items

        def ring_end(j):
            for half in range(2):
                total = partial(j, z, half)
                for way in range(2):
                    if comes(1, way, half):
                        ring[j, 1, way, half].wait_recv()
                        total = total + rb[j, way, 0, part(half), :].astype(F32)
                row_out[j, part(half), :] = total

        def reduce_first():
            copies = []
            for d in range(1, max(nx, ny)):
                if d < nx:
                    copies.append(send(w.at[0, peer("x", d)], r1.at[0, d - 1], x1s.at[0, d - 1], x1r.at[0, d - 1], "x", d))
                if d < ny:
                    copies.append(send(w.at[1, peer("y", d)], r1.at[1, d - 1], x1s.at[1, d - 1], x1r.at[1, d - 1], "y", d))
            return copies

        def sum_first():
            for ab in range(2):
                for n in range(minors[ab]):
                    total = w[ab, (x, y)[ab], n].astype(F32)
                    for d in range(majors[ab] - 1):
                        total = total + r1[ab, d, n].astype(F32)
                    t[ab, n] = total.astype(BF)

        def reduce_second():
            copies = []
            for d in range(1, max(nx, ny)):
                if d < ny:
                    copies.append(send(t.at[0, peer("y", d)], r2.at[0, d - 1], x2s.at[0, d - 1], x2r.at[0, d - 1], "y", d))
                if d < nx:
                    copies.append(send(t.at[1, peer("x", d)], r2.at[1, d - 1], x2s.at[1, d - 1], x2r.at[1, d - 1], "x", d))
            return copies

        def sum_second():
            for ab in range(2):
                total = t[ab, (y, x)[ab]].astype(F32)
                for d in range(minors[ab] - 1):
                    total = total + r2[ab, d].astype(F32)
                u[ab] = total.astype(BF).reshape(u.shape[1:])

        def reduce_third():
            return [
                send(u.at[:, peer("z", d)], r3.at[d - 1], x3s.at[d - 1], x3r.at[d - 1], "z", d)
                for d in range(1, nz)
            ]

        def sum_third():
            total = u[:, z].astype(F32)
            for d in range(nz - 1):
                total = total + r3[d].astype(F32)
            gz[:, z] = (total * scale).astype(BF)

        def gather_z():
            return [
                send(gz.at[:, z], gz.at[:, z], g0s.at[d - 1], g0r.at[d - 1], "z", d) for d in range(1, nz)
            ]

        def gather_minor():
            copies = []
            for d in range(1, max(nx, ny)):
                if d < ny:
                    copies.append(send(gz.at[0], g.at[c, 0, x, y], g1s.at[0, d - 1], g1r.at[0, d - 1], "y", d))
                if d < nx:
                    copies.append(send(gz.at[1], g.at[c, 1, y, x], g1s.at[1, d - 1], g1r.at[1, d - 1], "x", d))
            g[c, 0, x, y] = gz[0]
            g[c, 1, y, x] = gz[1]
            return copies

        def hand_over(ab, d):
            m = peer(("x", "y")[ab], -d)
            send(g.at[c, ab, m], g.at[c, ab, m], hs.at[ab, d], hr.at[ab, d], "core", 1)
            return local_copy(g.at[c, ab, m], g_out.at[c, ab, m], os.at[0, ab, d])

        def gather_major():
            copies = []
            for d in range(1, max(nx, ny)):
                if d < nx:
                    copies.append((0, d, send(g.at[c, 0, x], g.at[c, 0, x], g2s.at[0, d - 1], g2r.at[0, d - 1], "x", d)))
                if d < ny:
                    copies.append((1, d, send(g.at[c, 1, y], g.at[c, 1, y], g2s.at[1, d - 1], g2r.at[1, d - 1], "y", d)))
            return copies

        hop = first_hop(0)
        key_copy = send(keys, kbuf.at[c], ks.at[0], ks.at[1], "core", 1)
        kbuf[c] = keys[...]
        across = []
        for ab in range(2):
            for m in range(majors[ab]):
                block = term(other, ab, m, minors[ab]).astype(BF)
                for n in range(minors[ab]):
                    sw[ab, m, n] = block[:, n * 128 : (n + 1) * 128]
            across.append(send(sw.at[ab], rw.at[ab], ws.at[0, ab], ws.at[1, ab], "core", 1))
        arrived(*hop)
        hop = second_hop(0)
        for ab in range(2):
            across[ab].wait_recv()
            for m in range(majors[ab]):
                block = term(c, ab, m, minors[ab])
                for n in range(minors[ab]):
                    w[ab, m, n] = (block[:, n * 128 : (n + 1) * 128] + rw[ab, m, n].astype(F32)).astype(BF)
        arrived(*hop)
        shared = share_values(0)
        hop = first_hop(1)
        key_copy.wait_recv()
        shared.wait_recv()

        items = ring_items(0)
        per = 4
        for item in items[:2]:
            ring_item(*item)
        arrived(*hop)
        hop = second_hop(1)
        for item in items[2 : 2 + per]:
            ring_item(*item)
        arrived(*hop)
        shared = share_values(1)
        reduced = reduce_first()
        for item in items[2 + per :]:
            ring_item(*item)
        arrived(reduced)
        sum_first()
        reduced = reduce_second()
        ring_end(0)
        arrived(reduced)
        sum_second()
        reduced = reduce_third()
        shared.wait_recv()

        items = ring_items(1)
        for item in items[:2]:
            ring_item(*item)
        arrived(reduced)
        sum_third()
        gathered = gather_z()
        for item in items[2:4]:
            ring_item(*item)
        arrived(gathered)
        gathered = gather_minor()
        for item in items[4 : 2 + per]:
            ring_item(*item)
        arrived(gathered)
        gathered = gather_major()
        outs = [hand_over(ab, 0) for ab in range(2)]
        for item in items[2 + per :]:
            ring_item(*item)
        ring_end(1)
        for ab, d, copy in gathered:
            copy.wait_recv()
            outs.append(hand_over(ab, d))
        for ab in range(2):
            for d in range(majors[ab]):
                m = peer(("x", "y")[ab], -d)
                pltpu.make_async_remote_copy(
                    g.at[c, ab, m], g.at[other, ab, m], hs.at[ab, d], hr.at[ab, d],
                    device_id=device("core", 1), device_id_type=pl.DeviceIdType.MESH,
                ).wait_recv()
                outs.append(local_copy(g.at[other, ab, m], g_out.at[other, ab, m], os.at[1, ab, d]))
        for copy in outs:
            copy.wait()
        for copy in pending:
            copy.wait_send()

    return kernel


def exchange(nx, ny, nz, dp, inter, dpre, keys, rows, scale):
    samples, width = dp.shape[3:]
    pairs = inter.shape[1]
    quarter = pairs // 4
    far = nz // 2
    nm = max(nx, ny)
    dma = pltpu.SemaphoreType.DMA
    vmem = pltpu.VMEM
    scratch = [
        vmem((2, nx, ny, samples // 2, width), BF),
        vmem((2, ny, nx, samples // 2, width), BF),
        vmem((2, 2, nx, ny, samples, width), BF),
        vmem((2,) + keys.shape, jnp.int32),
        vmem((2, 2, far, rows, width), BF),
        vmem((2, 2, far, rows, width), BF),
        vmem((2, nm, nm, quarter, 128), BF),
        vmem((2, nm, nm, quarter, 128), BF),
        vmem((2, nm, nm, quarter, 128), BF),
        vmem((2, nm - 1, nm, quarter, 128), BF),
        vmem((2, nm, quarter, 128), BF),
        vmem((2, nm - 1, quarter, 128), BF),
        vmem((2, nz, quarter // nz, 128), BF),
        vmem((nz - 1, 2, quarter // nz, 128), BF),
        vmem((2, nz, quarter // nz, 128), BF),
        vmem((2, 2, nm, nm, nz, quarter // nz, 128), BF),
        dma((2,)),
        dma((2, 2, nm - 1)), dma((2, 2, nm - 1)), dma((2, 2, nm - 1)), dma((2, 2, nm - 1)),
        dma((2, 4)),
        dma((2, 2)),
        dma((2, 2, far, 2)), dma((2, 2, far, 2)),
        dma((2, 2)),
        dma((2, nm - 1)), dma((2, nm - 1)), dma((2, nm - 1)), dma((2, nm - 1)),
        dma((nz - 1,)), dma((nz - 1,)),
        dma((nz - 1,)), dma((nz - 1,)),
        dma((2, nm - 1)), dma((2, nm - 1)), dma((2, nm - 1)), dma((2, nm - 1)),
        dma((2, nm)), dma((2, nm)),
        dma((2, 2, nm)),
    ]
    in_vmem = pl.BlockSpec(memory_space=vmem)
    return pl.pallas_call(
        make_kernel(nx, ny, nz, samples, width, rows, scale),
        out_shape=(
            jax.ShapeDtypeStruct((2, 2, nm, nm, nz, quarter // nz, 128), BF),
            jax.ShapeDtypeStruct((2, rows, width), F32),
        ),
        in_specs=[in_vmem] * 4,
        out_specs=(pl.BlockSpec(memory_space=pl.ANY), in_vmem),
        scratch_shapes=scratch,
        compiler_params=pltpu.CompilerParams(
            collective_id=0, has_side_effects=True, vmem_limit_bytes=56 << 20
        ),
        name="exchange",
    )(dp, inter, dpre, keys)


def solution(mesh):
    nx = ny = math.isqrt(mesh.shape["group"])
    nz = mesh.shape["hash"] // 2
    fine = Mesh(mesh.devices.reshape(nx, ny, nz, 2), AXES)
    group, hashed = ("x", "y"), ("z", "core")

    def local(pooled, weight, cotangent, owners, local_rows, table, accum):
        vectors = pooled[0]
        samples, feats, width = vectors.shape
        rows = accum.shape[1]
        inter = jnp.einsum(
            "sfe,sge->sfg", vectors, vectors, preferred_element_type=F32
        ).astype(BF)
        inter_rows = inter.reshape(samples, feats * feats)
        preact = jnp.dot(inter_rows, weight, preferred_element_type=F32)
        sig = jax.nn.sigmoid(preact)
        dpre = (cotangent[0].astype(F32) * (sig * (1.0 + preact * (1.0 - sig)))).astype(BF)
        dinter = lax.dot_general(
            dpre, weight, (((1,), (1,)), ((), ())), preferred_element_type=F32
        ).reshape(samples, feats, feats)
        dsym = (dinter + jnp.swapaxes(dinter, 1, 2)).astype(BF)
        dpooled = jnp.einsum("sfg,sge->fse", dsym, vectors, preferred_element_type=F32).astype(BF)
        keys = owners[0] * rows + local_rows[0]
        keys = keys.reshape(2, nx, ny * samples, 2).transpose(1, 0, 3, 2).reshape(nx, 4, ny * samples)
        blocks, rowgrad = exchange(
            nx, ny, nz, dpooled.reshape(nx, ny, 2, samples, width), inter_rows, dpre, keys, rows,
            1.0 / math.sqrt(samples * nx * ny * nz * 2),
        )
        quarter = feats * feats // 4
        wgrad = (
            blocks.reshape(2, 2, nx, ny, quarter, 128).transpose(0, 1, 4, 2, 3, 5).reshape(weight.shape)
        )
        accum_out = accum + jnp.mean(rowgrad * rowgrad, axis=-1)
        table_out = table - 0.1 * rowgrad / jnp.sqrt(accum_out)[:, :, None]
        return (wgrad, table_out, accum_out)

    return jax.shard_map(
        local,
        mesh=fine,
        in_specs=(
            P(hashed, group, None, None),
            P(),
            P(hashed, group, None),
            P(hashed, group, None, None),
            P(hashed, group, None, None),
            P(group, hashed, None),
            P(group, hashed),
        ),
        out_specs=(P(), P(group, hashed, None), P(group, hashed)),
        check_vma=False,
    )
```

```python
import math

import jax
import jax.numpy as jnp
from jax import lax
from jax.experimental import pallas as pl
from jax.experimental.pallas import tpu as pltpu
from jax.sharding import Mesh, PartitionSpec as P

AXES = ("x", "y", "z", "core")
BF = jnp.bfloat16
F32 = jnp.float32


def make_kernel(nx, ny, nz, samples, width, rows, scale):
    far = nz // 2
    half_s = samples // 2
    half_r = rows // 2
    majors = (nx, ny)
    minors = (ny, nx)
    turns = 2 * far

    def kernel(
        dp, inter, dpre, keys, table, accum, wout, tout, aout,
        a1, v, kbuf, tot, sb, rb, sw, rw, w, wsb, wrb, s, r1, t, r2, gz,
        ks, f1s, f1r, f2s, f2r, loc, vs, vr, zs, zr, ws, wr, wzs, wzr,
        x1s, x1r, x2s, x2r, g0s, g0r, g1s, g1r, g2s, g2r, hs, hr,
    ):
        x, y, z, c = (lax.axis_index(a) for a in AXES)
        here = {"x": (x, nx), "y": (y, ny), "z": (z, nz), "core": (c, 2)}
        other = 1 - c

        def peer(axis, d):
            me, n = here[axis]
            return lax.rem(me + d + n, n)

        def remote(src, dst, ssem, rsem, axis, d):
            place = {a: here[a][0] for a in AXES}
            place[axis] = peer(axis, d)
            return pltpu.make_async_remote_copy(
                src, dst, ssem, rsem,
                device_id=tuple(place[a] for a in AXES), device_id_type=pl.DeviceIdType.MESH,
            )

        def start(copies):
            for copy in copies:
                copy.start()

        def arrived(copies):
            for copy in copies:
                copy.wait_recv()

        def left(copies):
            for copy in copies:
                copy.wait_send()

        barrier = pltpu.get_barrier_semaphore()
        greeted = 0
        for axis, n in (("core", 2), ("x", nx), ("y", ny), ("z", nz)):
            for d in range(1, n):
                place = {a: here[a][0] for a in AXES}
                place[axis] = peer(axis, d)
                pl.semaphore_signal(
                    barrier, inc=1, device_id=tuple(place[a] for a in AXES),
                    device_id_type=pl.DeviceIdType.MESH,
                )
                greeted += 1
        pl.semaphore_wait(barrier, greeted)

        firsts, seconds = ("x", "y"), ("y", "x")
        lead, trail = (x, y), (y, x)

        def piece(ab, p, q, j):
            p, q = (p, q) if ab == 0 else (q, p)
            return dp.at[p, q, j, pl.ds(ab * half_s, half_s), :]

        def place_of(ab, p, q, j):
            p, q = (p, q) if ab == 0 else (q, p)
            return v.at[j, c, p, q, pl.ds(ab * half_s, half_s), :]

        def hop_direct(j, ab):
            return [
                remote(
                    piece(ab, lead[ab], peer(seconds[ab], e), j), place_of(ab, lead[ab], trail[ab], j),
                    f2s.at[j, ab, 0, e - 1], f2r.at[j, ab, 0, e - 1], seconds[ab], e,
                )
                for e in range(1, minors[ab])
            ]

        def hop_first(j, ab, e):
            copies = []
            for d in range(1, majors[ab]):
                q = peer(seconds[ab], e)
                src = piece(ab, peer(firsts[ab], d), q, j)
                dst = place_of(ab, lead[ab], trail[ab], j) if e == 0 else a1.at[j, ab, d - 1, e - 1]
                copies.append(remote(
                    src, dst, f1s.at[j, ab, d - 1, e], f1r.at[j, ab, d - 1, e], firsts[ab], d,
                ))
            return copies

        def hop_second(j, ab, d, e):
            origin = peer(firsts[ab], -d)
            return remote(
                a1.at[j, ab, d - 1, e - 1], place_of(ab, origin, trail[ab], j),
                f2s.at[j, ab, d, e - 1], f2r.at[j, ab, d, e - 1], seconds[ab], e,
            )

        def own_pieces(j):
            return [
                pltpu.make_async_copy(
                    piece(ab, lead[ab], trail[ab], j), place_of(ab, lead[ab], trail[ab], j), loc.at[j, ab]
                )
                for ab in range(2)
            ]

        def hop_start(j):
            for e in range(1, max(nx, ny)):
                for ab in range(2):
                    if e < minors[ab]:
                        start(hop_first(j, ab, e))
            for ab in range(2):
                start(hop_direct(j, ab))
            for ab in range(2):
                start(hop_first(j, ab, 0))
            start(own_pieces(j))

        def hop_forward(j):
            for e in range(1, max(nx, ny)):
                for ab in range(2):
                    if e < minors[ab]:
                        for d, copy in enumerate(hop_first(j, ab, e), 1):
                            copy.wait_recv()
                            hop_second(j, ab, d, e).start()

        def share(j, p):
            return remote(
                v.at[j, c, p], v.at[j, c, p], vs.at[j, p], vr.at[j, p], "core", 1
            )

        def hop_end(j):
            for copy in own_pieces(j):
                copy.wait()
            for ab in range(2):
                arrived(hop_direct(j, ab))
                arrived(hop_first(j, ab, 0))
            for ab in range(2):
                for d in range(1, majors[ab]):
                    for e in range(1, minors[ab]):
                        hop_second(j, ab, d, e).wait_recv()
            for p in range(nx):
                share(j, p).start()

        def shared(j):
            for p in range(nx):
                share(j, p).wait_recv()

        def hop_left(j):
            for ab in range(2):
                left(hop_direct(j, ab))
                for e in range(minors[ab]):
                    left(hop_first(j, ab, e))
                for d in range(1, majors[ab]):
                    left([hop_second(j, ab, d, e) for e in range(1, minors[ab])])
            left([share(j, p) for p in range(nx)])

        def key_copy():
            return remote(keys, kbuf.at[c], ks.at[0], ks.at[1], "core", 1)

        def term(core, ab, m):
            r = nz * w.shape[4]
            cols = minors[ab] * 128
            return lax.dot_general(
                inter[:, pl.ds(pl.multiple_of((core * 2 + ab) * r, 128), r)],
                dpre[:, m * cols : (m + 1) * cols],
                (((0,), (0,)), ((), ())),
                preferred_element_type=F32,
            )

        def term_into(ref, core, ab):
            b = w.shape[4]
            for m in range(majors[ab]):
                block = term(core, ab, m).astype(ref.dtype)
                for n in range(minors[ab]):
                    for q in range(nz):
                        ref[ab, q, m, n] = block[q * b : (q + 1) * b, n * 128 : (n + 1) * 128]

        def term_across(ab):
            return remote(sw.at[ab], rw.at[ab], ws.at[ab], wr.at[ab], "core", 1)

        def toward(way, k):
            return peer("z", k if way == 0 else -k)

        def comes(k, way, half):
            return k < far or (k == far and way == half)

        def weight_copy(k, way, half):
            return remote(
                wsb.at[way, k - 1, half], wrb.at[way, k - 1, half],
                wzs.at[way, k - 1, half], wzr.at[way, k - 1, half], "z", 1 if way == 0 else -1,
            )

        def weight_step(k):
            for way, half in ((0, 0), (1, 1), (0, 1), (1, 0)):
                if comes(k, way, half):
                    dest = toward(way, k)
                    total = w[half, dest] + rw[half, dest].astype(F32)
                    if comes(k + 1, way, half):
                        weight_copy(k + 1, way, half).wait_recv()
                        total = total + wrb[way, k, half].astype(F32)
                    wsb[way, k - 1, half] = total.astype(BF)
                    weight_copy(k, way, half).start()

        def weight_end():
            for half in range(2):
                total = w[half, z] + rw[half, z].astype(F32)
                for way in range(2):
                    if comes(1, way, half):
                        weight_copy(1, way, half).wait_recv()
                        total = total + wrb[way, 0, half].astype(F32)
                s[half] = total

        def weight_left():
            for k in range(1, far + 1):
                for way in range(2):
                    for half in range(2):
                        if comes(k, way, half):
                            weight_copy(k, way, half).wait_send()

        def reduce_first():
            return [
                remote(
                    s.at[ab, peer(firsts[ab], d)], r1.at[ab, d - 1],
                    x1s.at[ab, d - 1], x1r.at[ab, d - 1], firsts[ab], d,
                )
                for ab in range(2) for d in range(1, majors[ab])
            ]

        def sum_first():
            for ab in range(2):
                total = s[ab, lead[ab]]
                for d in range(majors[ab] - 1):
                    total = total + r1[ab, d]
                t[ab] = total

        def reduce_second():
            return [
                remote(
                    t.at[ab, peer(seconds[ab], d)], r2.at[ab, d - 1],
                    x2s.at[ab, d - 1], x2r.at[ab, d - 1], seconds[ab], d,
                )
                for ab in range(2) for d in range(1, minors[ab])
            ]

        piece_rows = w.shape[4]
        quarter = nz * piece_rows

        def my_rows():
            return pl.ds(pl.multiple_of(z * piece_rows, 16), piece_rows)

        def sum_second():
            for ab in range(2):
                total = t[ab, trail[ab]]
                for d in range(minors[ab] - 1):
                    total = total + r2[ab, d]
                gz[ab, my_rows(), :] = (total * scale).astype(BF)

        def gather_z():
            return [
                remote(
                    gz.at[:, my_rows(), :], gz.at[:, my_rows(), :], g0s.at[d - 1], g0r.at[d - 1], "z", d
                )
                for d in range(1, nz)
            ]

        def out_block(core, ab, m, n=None):
            r = pl.ds(pl.multiple_of((core * 2 + ab) * quarter, 16), quarter)
            if n is None:
                cols = pl.ds(pl.multiple_of(m * (minors[ab] * 128), 128), minors[ab] * 128)
            else:
                cols = pl.ds(pl.multiple_of((m * minors[ab] + n) * 128, 128), 128)
            return r, cols

        def gather_minor():
            copies = []
            for ab in range(2):
                r, cols = out_block(c, ab, lead[ab], trail[ab])
                copies += [
                    remote(gz.at[ab], wout.at[r, cols], g1s.at[ab, d - 1], g1r.at[ab, d - 1], seconds[ab], d)
                    for d in range(1, minors[ab])
                ]
            return copies

        def keep_minor():
            for ab in range(2):
                r, cols = out_block(c, ab, lead[ab], trail[ab])
                wout[r, cols] = gz[ab]

        def gather_major(ab):
            r, cols = out_block(c, ab, lead[ab])
            return [
                remote(wout.at[r, cols], wout.at[r, cols], g2s.at[ab, d - 1], g2r.at[ab, d - 1], firsts[ab], d)
                for d in range(1, majors[ab])
            ]

        def hand_over(ab, d):
            r, cols = out_block(c, ab, peer(firsts[ab], -d))
            return remote(wout.at[r, cols], wout.at[r, cols], hs.at[ab, d], hr.at[ab, d], "core", 1)

        def partial(j, dest):
            base = (2 * dest + c) * rows
            iota = lax.broadcasted_iota(jnp.int32, (rows, ny * samples), 0).astype(jnp.int16)
            acc = None
            for q in range(2 * nx):
                h = c if q < nx else other
                i = q % nx
                first = (kbuf[h, i, pl.ds(2 * j, 1), :] - base).astype(jnp.int16)
                second = (kbuf[h, i, pl.ds(2 * j + 1, 1), :] - base).astype(jnp.int16)
                hot = jnp.where((iota == first) | (iota == second), BF(1), BF(0))
                prod = jnp.dot(
                    hot, v[j, h, i].reshape(ny * samples, width), preferred_element_type=F32
                )
                acc = prod if acc is None else acc + prod
            tot[...] = acc

        def part(half):
            return pl.ds(half * half_r, half_r)

        def ring_copy(j, k, way, half):
            step = 1 - 2 * way
            return remote(
                sb.at[j, way, k - 1, part(half), :], rb.at[j, way, k - 1, part(half), :],
                zs.at[j, way, k - 1, half], zr.at[j, way, k - 1, half], "z", step,
            )

        def turn(step):
            j = step // turns
            i = lax.rem(step, turns)
            k = far - (i + 1) // 2
            way = lax.rem(i + 1, 2)
            partial(j, peer("z", k * (1 - 2 * way)))

            @pl.when(i == 0)
            def _():
                for half in range(2):
                    sb[j, half, far - 1, part(half), :] = tot[part(half), :].astype(BF)
                    ring_copy(j, far, half, half).start()

            for near in (True, False):
                @pl.when(jnp.logical_and(i > 0, i < turns - 1) & ((k < far - 1) if near else (k == far - 1)))
                def _():
                    for half in range(2):
                        if near:
                            ring_copy(j, k + 1, way, half).wait_recv()
                            sb[j, way, k - 1, part(half), :] = (
                                tot[part(half), :] + rb[j, way, k, part(half), :].astype(F32)
                            ).astype(BF)
                        else:
                            @pl.when(way == half)
                            def _():
                                ring_copy(j, far, half, half).wait_recv()
                                sb[j, way, k - 1, part(half), :] = (
                                    tot[part(half), :] + rb[j, half, far - 1, part(half), :].astype(F32)
                                ).astype(BF)

                            @pl.when(way != half)
                            def _():
                                sb[j, way, k - 1, part(half), :] = tot[part(half), :].astype(BF)
                        ring_copy(j, k, way, half).start()

            @pl.when(i == turns - 1)
            def _():
                for half in range(2):
                    for w_ in range(2):
                        if comes(1, w_, half):
                            ring_copy(j, 1, w_, half).wait_recv()
                rowgrad = tot[...]
                if far > 1:
                    rowgrad = rowgrad + rb[j, 0, 0].astype(F32) + rb[j, 1, 0].astype(F32)
                else:
                    rowgrad = rowgrad + jnp.concatenate(
                        [rb[j, 0, 0, part(0), :], rb[j, 1, 0, part(1), :]], axis=0
                    ).astype(F32)
                old = jnp.transpose(jnp.broadcast_to(accum[pl.ds(j, 1), :], (128, rows)))[:, 0:1]
                new = old + jnp.sum(rowgrad * rowgrad, axis=1, keepdims=True) * (1.0 / width)
                aout[pl.ds(j, 1), :] = jnp.transpose(jnp.broadcast_to(new, (rows, 128)))[0:1, :]
                tout[j] = table[j] - 0.1 * rowgrad / jnp.sqrt(new)

        def ring_left():
            for j in range(2):
                for k in range(1, far + 1):
                    for way in range(2):
                        for half in range(2):
                            if comes(k, way, half):
                                ring_copy(j, k, way, half).wait_send()

        hop_start(0)
        key_copy().start()
        kbuf[c] = keys[...]
        for ab in range(2):
            term_into(sw, other, ab)
            term_across(ab).start()
        for ab in range(2):
            term_into(w, c, ab)
        arrived([term_across(ab) for ab in range(2)])
        weight_step(far)
        hop_forward(0)
        for k in range(far - 1, 1, -1):
            weight_step(k)
        hop_end(0)
        hop_start(1)
        if far > 1:
            weight_step(1)
        key_copy().wait_recv()
        shared(0)

        def finish_second():
            arrived(reduce_second())
            sum_second()
            start(gather_z())

        def begin_reduce():
            weight_end()
            start(reduce_first())

        def middle_reduce():
            arrived(reduce_first())
            sum_first()
            start(reduce_second())

        def begin_gather():
            arrived(gather_z())
            start(gather_minor())
            keep_minor()

        def begin_major():
            arrived(gather_minor())
            for ab in range(2):
                start(gather_major(ab))
                hand_over(ab, 0).start()

        def hand_on():
            for ab in range(2):
                arrived(gather_major(ab))
                for d in range(1, majors[ab]):
                    hand_over(ab, d).start()

        tasks = [
            (1, begin_reduce), (2, lambda: hop_forward(1)), (3, middle_reduce), (4, finish_second),
            (5, lambda: hop_end(1)), (5, begin_gather), (6, begin_major), (7, lambda: shared(1)),
            (13, hand_on),
        ]

        def body(step, carry):
            turn(step)
            for at, task in tasks:
                pl.when(step == at * turns // 8)(task)
            return carry

        lax.fori_loop(0, 2 * turns, body, 0)

        for ab in range(2):
            for d in range(majors[ab]):
                hand_over(ab, d).wait_recv()
        for j in range(2):
            hop_left(j)
        left([key_copy()] + [term_across(ab) for ab in range(2)])
        weight_left()
        ring_left()
        left(reduce_first() + reduce_second() + gather_z() + gather_minor())
        for ab in range(2):
            left(gather_major(ab) + [hand_over(ab, d) for d in range(majors[ab])])

    return kernel


def exchange(nx, ny, nz, dp, inter, dpre, keys, table, accum, scale):
    samples, width = dp.shape[3:]
    rows = accum.shape[1]
    pairs, hidden = inter.shape[1], dpre.shape[1]
    b = pairs // 4 // nz
    far = nz // 2
    nm = max(nx, ny)
    dma = pltpu.SemaphoreType.DMA
    vmem = pltpu.VMEM
    scratch = [
        vmem((2, 2, nm - 1, nm - 1, samples // 2, width), BF),
        vmem((2, 2, nx, ny, samples, width), BF),
        vmem((2,) + keys.shape, jnp.int32),
        vmem((rows, width), F32),
        vmem((2, 2, far, rows, width), BF),
        vmem((2, 2, far, rows, width), BF),
        vmem((2, nz, nm, nm, b, 128), BF),
        vmem((2, nz, nm, nm, b, 128), BF),
        vmem((2, nz, nm, nm, b, 128), F32),
        vmem((2, far, 2, nm, nm, b, 128), BF),
        vmem((2, far, 2, nm, nm, b, 128), BF),
        vmem((2, nm, nm, b, 128), F32),
        vmem((2, nm - 1, nm, b, 128), F32),
        vmem((2, nm, b, 128), F32),
        vmem((2, nm - 1, b, 128), F32),
        vmem((2, nz * b, 128), BF),
        dma((2,)),
        dma((2, 2, nm - 1, nm)), dma((2, 2, nm - 1, nm)),
        dma((2, 2, nm, nm - 1)), dma((2, 2, nm, nm - 1)),
        dma((2, 2)),
        dma((2, nx)), dma((2, nx)),
        dma((2, 2, far, 2)), dma((2, 2, far, 2)),
        dma((2,)), dma((2,)),
        dma((2, far, 2)), dma((2, far, 2)),
        dma((2, nm - 1)), dma((2, nm - 1)), dma((2, nm - 1)), dma((2, nm - 1)),
        dma((nz - 1,)), dma((nz - 1,)),
        dma((2, nm - 1)), dma((2, nm - 1)), dma((2, nm - 1)), dma((2, nm - 1)),
        dma((2, nm)), dma((2, nm)),
    ]
    in_vmem = pl.BlockSpec(memory_space=vmem)
    return pl.pallas_call(
        make_kernel(nx, ny, nz, samples, width, rows, scale),
        out_shape=(
            jax.ShapeDtypeStruct((pairs, hidden), BF),
            jax.ShapeDtypeStruct(table.shape, F32),
            jax.ShapeDtypeStruct(accum.shape, F32),
        ),
        in_specs=[in_vmem] * 6,
        out_specs=(in_vmem,) * 3,
        scratch_shapes=scratch,
        compiler_params=pltpu.CompilerParams(
            collective_id=0, has_side_effects=True, vmem_limit_bytes=56 << 20
        ),
        name="exchange",
    )(dp, inter, dpre, keys, table, accum)


def solution(mesh):
    nx = ny = math.isqrt(mesh.shape["group"])
    nz = mesh.shape["hash"] // 2
    fine = Mesh(mesh.devices.reshape(nx, ny, nz, 2), AXES)
    group, hashed = ("x", "y"), ("z", "core")

    def local(pooled, weight, cotangent, owners, local_rows, table, accum):
        vectors = pooled[0]
        samples, feats, width = vectors.shape
        rows = accum.shape[1]
        inter = jnp.einsum(
            "sfe,sge->sfg", vectors, vectors, preferred_element_type=F32
        ).astype(BF)
        inter_rows = inter.reshape(samples, feats * feats)
        preact = jnp.dot(inter_rows, weight, preferred_element_type=F32)
        sig = jax.nn.sigmoid(preact)
        dpre = (cotangent[0].astype(F32) * (sig * (1.0 + preact * (1.0 - sig)))).astype(BF)
        dinter = lax.dot_general(
            dpre, weight, (((1,), (1,)), ((), ())), preferred_element_type=F32
        ).reshape(samples, feats, feats)
        dsym = (dinter + jnp.swapaxes(dinter, 1, 2)).astype(BF)
        dpooled = jnp.einsum("sfg,sge->fse", dsym, vectors, preferred_element_type=F32).astype(BF)
        keys = owners[0] * rows + local_rows[0]
        keys = keys.reshape(2, nx, ny * samples, 2).transpose(1, 0, 3, 2).reshape(nx, 4, ny * samples)
        return exchange(
            nx, ny, nz, dpooled.reshape(nx, ny, 2, samples, width), inter_rows, dpre, keys, table, accum,
            1.0 / math.sqrt(samples * nx * ny * nz * 2),
        )

    return jax.shard_map(
        local,
        mesh=fine,
        in_specs=(
            P(hashed, group, None, None),
            P(),
            P(hashed, group, None),
            P(hashed, group, None, None),
            P(hashed, group, None, None),
            P(group, hashed, None),
            P(group, hashed),
        ),
        out_specs=(P(), P(group, hashed, None), P(group, hashed)),
        check_vma=False,
    )
```

```python
import math

import jax
import jax.numpy as jnp
from jax import lax
from jax.experimental import pallas as pl
from jax.experimental.pallas import tpu as pltpu
from jax.sharding import Mesh, PartitionSpec as P

AXES = ("x", "y", "z", "core")
BF = jnp.bfloat16
F32 = jnp.float32


def make_kernel(nx, ny, nz, samples, width, rows, scale):
    far = nz // 2
    half_s = samples // 2
    half_r = rows // 2
    majors = (nx, ny)
    minors = (ny, nx)

    def kernel(
        dp, inter, dpre, keys, table, accum, wout, tout, aout,
        a1, v, kbuf, tot, sb, rb, sw, rw, w, wsb, wrb, s, r1, t, r2, gz,
        ks, f1s, f1r, f2s, f2r, loc, vs, vr, zs, zr, ws, wr, wzs, wzr,
        x1s, x1r, x2s, x2r, g0s, g0r, g1s, g1r, g2s, g2r, hs, hr,
    ):
        x, y, z, c = (lax.axis_index(a) for a in AXES)
        here = {"x": (x, nx), "y": (y, ny), "z": (z, nz), "core": (c, 2)}
        other = 1 - c

        def peer(axis, d):
            me, n = here[axis]
            return lax.rem(me + d + n, n)

        def remote(src, dst, ssem, rsem, axis, d):
            place = {a: here[a][0] for a in AXES}
            place[axis] = peer(axis, d)
            return pltpu.make_async_remote_copy(
                src, dst, ssem, rsem,
                device_id=tuple(place[a] for a in AXES), device_id_type=pl.DeviceIdType.MESH,
            )

        def start(copies):
            for copy in copies:
                copy.start()

        def arrived(copies):
            for copy in copies:
                copy.wait_recv()

        def left(copies):
            for copy in copies:
                copy.wait_send()

        barrier = pltpu.get_barrier_semaphore()
        greeted = 0
        for axis, n in (("core", 2), ("x", nx), ("y", ny), ("z", nz)):
            for d in range(1, n):
                place = {a: here[a][0] for a in AXES}
                place[axis] = peer(axis, d)
                pl.semaphore_signal(
                    barrier, inc=1, device_id=tuple(place[a] for a in AXES),
                    device_id_type=pl.DeviceIdType.MESH,
                )
                greeted += 1
        pl.semaphore_wait(barrier, greeted)

        firsts, seconds = ("x", "y"), ("y", "x")
        lead, trail = (x, y), (y, x)

        def piece(ab, p, q, j):
            p, q = (p, q) if ab == 0 else (q, p)
            return dp.at[p, q, j, pl.ds(ab * half_s, half_s), :]

        def place_of(ab, p, q, j):
            p, q = (p, q) if ab == 0 else (q, p)
            return v.at[j, c, p, q, pl.ds(ab * half_s, half_s), :]

        def hop_direct(j, ab):
            return [
                remote(
                    piece(ab, lead[ab], peer(seconds[ab], e), j), place_of(ab, lead[ab], trail[ab], j),
                    f2s.at[j, ab, 0, e - 1], f2r.at[j, ab, 0, e - 1], seconds[ab], e,
                )
                for e in range(1, minors[ab])
            ]

        def hop_first(j, ab, e):
            copies = []
            for d in range(1, majors[ab]):
                q = peer(seconds[ab], e)
                src = piece(ab, peer(firsts[ab], d), q, j)
                dst = place_of(ab, lead[ab], trail[ab], j) if e == 0 else a1.at[j, ab, d - 1, e - 1]
                copies.append(remote(
                    src, dst, f1s.at[j, ab, d - 1, e], f1r.at[j, ab, d - 1, e], firsts[ab], d,
                ))
            return copies

        def hop_second(j, ab, d, e):
            origin = peer(firsts[ab], -d)
            return remote(
                a1.at[j, ab, d - 1, e - 1], place_of(ab, origin, trail[ab], j),
                f2s.at[j, ab, d, e - 1], f2r.at[j, ab, d, e - 1], seconds[ab], e,
            )

        def own_pieces(j):
            return [
                pltpu.make_async_copy(
                    piece(ab, lead[ab], trail[ab], j), place_of(ab, lead[ab], trail[ab], j), loc.at[j, ab]
                )
                for ab in range(2)
            ]

        def hop_start(j):
            for e in range(1, max(nx, ny)):
                for ab in range(2):
                    if e < minors[ab]:
                        start(hop_first(j, ab, e))
            for ab in range(2):
                start(hop_direct(j, ab))
            for ab in range(2):
                start(hop_first(j, ab, 0))
            start(own_pieces(j))

        def hop_forward(j):
            for e in range(1, max(nx, ny)):
                for ab in range(2):
                    if e < minors[ab]:
                        for d, copy in enumerate(hop_first(j, ab, e), 1):
                            copy.wait_recv()
                            hop_second(j, ab, d, e).start()

        def share(j, p):
            return remote(
                v.at[j, c, p], v.at[j, c, p], vs.at[j, p], vr.at[j, p], "core", 1
            )

        def hop_end(j):
            for copy in own_pieces(j):
                copy.wait()
            for ab in range(2):
                arrived(hop_direct(j, ab))
                arrived(hop_first(j, ab, 0))
            for ab in range(2):
                for d in range(1, majors[ab]):
                    for e in range(1, minors[ab]):
                        hop_second(j, ab, d, e).wait_recv()
            for p in range(nx):
                share(j, p).start()

        def shared(j):
            for p in range(nx):
                share(j, p).wait_recv()

        def hop_left(j):
            for ab in range(2):
                left(hop_direct(j, ab))
                for e in range(minors[ab]):
                    left(hop_first(j, ab, e))
                for d in range(1, majors[ab]):
                    left([hop_second(j, ab, d, e) for e in range(1, minors[ab])])
            left([share(j, p) for p in range(nx)])

        def key_copy():
            return remote(keys, kbuf.at[c], ks.at[0], ks.at[1], "core", 1)

        def term(core, ab, m):
            r = nz * w.shape[4]
            cols = minors[ab] * 128
            return lax.dot_general(
                inter[:, pl.ds(pl.multiple_of((core * 2 + ab) * r, 128), r)],
                dpre[:, m * cols : (m + 1) * cols],
                (((0,), (0,)), ((), ())),
                preferred_element_type=F32,
            )

        def term_into(ref, core, ab):
            b = w.shape[4]
            for m in range(majors[ab]):
                block = term(core, ab, m).astype(ref.dtype)
                for n in range(minors[ab]):
                    for q in range(nz):
                        ref[ab, q, m, n] = block[q * b : (q + 1) * b, n * 128 : (n + 1) * 128]

        def term_across(ab):
            return remote(sw.at[ab], rw.at[ab], ws.at[ab], wr.at[ab], "core", 1)

        def toward(way, k):
            return peer("z", k if way == 0 else -k)

        def comes(k, way, half):
            return k < far or (k == far and way == half)

        def weight_copy(k, way, half):
            return remote(
                wsb.at[way, k - 1, half], wrb.at[way, k - 1, half],
                wzs.at[way, k - 1, half], wzr.at[way, k - 1, half], "z", 1 if way == 0 else -1,
            )

        def weight_step(k):
            for way, half in ((0, 0), (1, 1), (0, 1), (1, 0)):
                if comes(k, way, half):
                    dest = toward(way, k)
                    total = w[half, dest] + rw[half, dest].astype(F32)
                    if comes(k + 1, way, half):
                        weight_copy(k + 1, way, half).wait_recv()
                        total = total + wrb[way, k, half].astype(F32)
                    wsb[way, k - 1, half] = total.astype(BF)
                    weight_copy(k, way, half).start()

        def weight_end():
            for half in range(2):
                total = w[half, z] + rw[half, z].astype(F32)
                for way in range(2):
                    if comes(1, way, half):
                        weight_copy(1, way, half).wait_recv()
                        total = total + wrb[way, 0, half].astype(F32)
                s[half] = total

        def weight_left():
            for k in range(1, far + 1):
                for way in range(2):
                    for half in range(2):
                        if comes(k, way, half):
                            weight_copy(k, way, half).wait_send()

        def reduce_first():
            return [
                remote(
                    s.at[ab, peer(firsts[ab], d)], r1.at[ab, d - 1],
                    x1s.at[ab, d - 1], x1r.at[ab, d - 1], firsts[ab], d,
                )
                for ab in range(2) for d in range(1, majors[ab])
            ]

        def sum_first():
            for ab in range(2):
                total = s[ab, lead[ab]]
                for d in range(majors[ab] - 1):
                    total = total + r1[ab, d]
                t[ab] = total

        def reduce_second():
            return [
                remote(
                    t.at[ab, peer(seconds[ab], d)], r2.at[ab, d - 1],
                    x2s.at[ab, d - 1], x2r.at[ab, d - 1], seconds[ab], d,
                )
                for ab in range(2) for d in range(1, minors[ab])
            ]

        piece_rows = w.shape[4]
        quarter = nz * piece_rows

        def my_rows():
            return pl.ds(pl.multiple_of(z * piece_rows, 16), piece_rows)

        def sum_second():
            for ab in range(2):
                total = t[ab, trail[ab]]
                for d in range(minors[ab] - 1):
                    total = total + r2[ab, d]
                gz[ab, my_rows(), :] = (total * scale).astype(BF)

        def gather_z():
            return [
                remote(
                    gz.at[:, my_rows(), :], gz.at[:, my_rows(), :], g0s.at[d - 1], g0r.at[d - 1], "z", d
                )
                for d in range(1, nz)
            ]

        def out_block(core, ab, m, n=None):
            r = pl.ds(pl.multiple_of((core * 2 + ab) * quarter, 16), quarter)
            if n is None:
                cols = pl.ds(pl.multiple_of(m * (minors[ab] * 128), 128), minors[ab] * 128)
            else:
                cols = pl.ds(pl.multiple_of((m * minors[ab] + n) * 128, 128), 128)
            return r, cols

        def gather_minor():
            copies = []
            for ab in range(2):
                r, cols = out_block(c, ab, lead[ab], trail[ab])
                copies += [
                    remote(gz.at[ab], wout.at[r, cols], g1s.at[ab, d - 1], g1r.at[ab, d - 1], seconds[ab], d)
                    for d in range(1, minors[ab])
                ]
            return copies

        def keep_minor():
            for ab in range(2):
                r, cols = out_block(c, ab, lead[ab], trail[ab])
                wout[r, cols] = gz[ab]

        def gather_major(ab):
            r, cols = out_block(c, ab, lead[ab])
            return [
                remote(wout.at[r, cols], wout.at[r, cols], g2s.at[ab, d - 1], g2r.at[ab, d - 1], firsts[ab], d)
                for d in range(1, majors[ab])
            ]

        def hand_over(ab, d):
            r, cols = out_block(c, ab, peer(firsts[ab], -d))
            return remote(wout.at[r, cols], wout.at[r, cols], hs.at[ab, d], hr.at[ab, d], "core", 1)

        def partial(j, dest, slot):
            base = (2 * dest + c) * rows
            iota = lax.broadcasted_iota(jnp.int32, (rows, ny * samples), 0).astype(jnp.int16)
            acc = None
            for q in range(2 * nx):
                h = c if q < nx else other
                i = q % nx
                first = (kbuf[h, i, pl.ds(2 * j, 1), :] - base).astype(jnp.int16)
                second = (kbuf[h, i, pl.ds(2 * j + 1, 1), :] - base).astype(jnp.int16)
                hot = jnp.where((iota == first) | (iota == second), BF(1), BF(0))
                prod = jnp.dot(
                    hot, v[j, h, i].reshape(ny * samples, width), preferred_element_type=F32
                )
                acc = prod if acc is None else acc + prod
            tot[slot] = acc

        def part(half):
            return pl.ds(half * half_r, half_r)

        def ring_copy(j, k, way, half):
            step = 1 - 2 * way
            return remote(
                sb.at[j, way, k - 1, part(half), :], rb.at[j, way, k - 1, part(half), :],
                zs.at[j, way, k - 1, half], zr.at[j, way, k - 1, half], "z", step,
            )

        def turn(step):
            early = step < far
            j = jnp.where(early | (step == far + 1), 0, 1)
            k = jnp.where(early, far - step, 2 * far + 1 - step)
            k = jnp.where(step == far, far, jnp.where(step == far + 1, 0, k))

            def one(way, carry):
                partial(j, peer("z", k * (1 - 2 * way)), way)
                return carry

            lax.fori_loop(0, jnp.where((k == 0) | (k == far), 1, 2), one, 0)

            @pl.when(k == far)
            def _():
                for half in range(2):
                    sb[j, half, far - 1, part(half), :] = tot[0, part(half), :].astype(BF)
                    ring_copy(j, far, half, half).start()

            if far > 1:
                @pl.when((k > 0) & (k < far))
                def _():
                    for way, half in ((0, 0), (1, 1)):
                        ring_copy(j, k + 1, way, half).wait_recv()
                        sb[j, way, k - 1, part(half), :] = (
                            tot[way, part(half), :] + rb[j, way, k, part(half), :].astype(F32)
                        ).astype(BF)
                        ring_copy(j, k, way, half).start()

                @pl.when(k == far - 1)
                def _():
                    for way, half in ((0, 1), (1, 0)):
                        sb[j, way, far - 2, part(half), :] = tot[way, part(half), :].astype(BF)
                        ring_copy(j, far - 1, way, half).start()

            if far > 2:
                @pl.when((k > 0) & (k < far - 1))
                def _():
                    for way, half in ((0, 1), (1, 0)):
                        ring_copy(j, k + 1, way, half).wait_recv()
                        sb[j, way, k - 1, part(half), :] = (
                            tot[way, part(half), :] + rb[j, way, k, part(half), :].astype(F32)
                        ).astype(BF)
                        ring_copy(j, k, way, half).start()

            @pl.when(k == 0)
            def _():
                for half in range(2):
                    for w_ in range(2):
                        if comes(1, w_, half):
                            ring_copy(j, 1, w_, half).wait_recv()
                rowgrad = tot[0]
                if far > 1:
                    rowgrad = rowgrad + rb[j, 0, 0].astype(F32) + rb[j, 1, 0].astype(F32)
                else:
                    rowgrad = rowgrad + jnp.concatenate(
                        [rb[j, 0, 0, part(0), :], rb[j, 1, 0, part(1), :]], axis=0
                    ).astype(F32)
                old = jnp.transpose(jnp.broadcast_to(accum[pl.ds(j, 1), :], (128, rows)))[:, 0:1]
                new = old + jnp.sum(rowgrad * rowgrad, axis=1, keepdims=True) * (1.0 / width)
                aout[pl.ds(j, 1), :] = jnp.transpose(jnp.broadcast_to(new, (rows, 128)))[0:1, :]
                tout[j] = table[j] - 0.1 * rowgrad / jnp.sqrt(new)

        def ring_left():
            for j in range(2):
                for k in range(1, far + 1):
                    for way in range(2):
                        for half in range(2):
                            if comes(k, way, half):
                                ring_copy(j, k, way, half).wait_send()

        hop_start(0)
        key_copy().start()
        kbuf[c] = keys[...]
        for ab in range(2):
            term_into(sw, other, ab)
            term_across(ab).start()
        for ab in range(2):
            term_into(w, c, ab)
        arrived([term_across(ab) for ab in range(2)])
        weight_step(far)
        hop_forward(0)
        if far > 1:
            weight_step(far - 1)
        hop_end(0)
        hop_start(1)
        key_copy().wait_recv()
        shared(0)

        def late_steps(last):
            for k in range(far - 2, 0, -1):
                if (k == 1) == last:
                    weight_step(k)

        def finish_second():
            arrived(reduce_second())
            sum_second()
            start(gather_z())

        def begin_reduce():
            weight_end()
            start(reduce_first())

        def middle_reduce():
            arrived(reduce_first())
            sum_first()
            start(reduce_second())

        def begin_gather():
            arrived(gather_z())
            start(gather_minor())
            keep_minor()

        def begin_major():
            arrived(gather_minor())
            for ab in range(2):
                start(gather_major(ab))
                hand_over(ab, 0).start()

        def hand_on():
            for ab in range(2):
                arrived(gather_major(ab))
                for d in range(1, majors[ab]):
                    hand_over(ab, d).start()

        tasks = (
            [lambda: late_steps(False)],
            [lambda: late_steps(True), lambda: hop_forward(1)],
            [begin_reduce],
            [lambda: hop_end(1), middle_reduce, lambda: shared(1)],
            [finish_second],
            [begin_gather],
            [begin_major],
            [],
            [hand_on],
        )

        def body(step, carry):
            turn(step)
            for at, group in enumerate(tasks):
                for task in group:
                    pl.when(step == (min(at, far - 1) if at < 4 else min(at - 4 + far, 2 * far + 1)))(task)
            return carry

        lax.fori_loop(0, 2 * (far + 1), body, 0)

        for ab in range(2):
            for d in range(majors[ab]):
                hand_over(ab, d).wait_recv()
        for j in range(2):
            hop_left(j)
        left([key_copy()] + [term_across(ab) for ab in range(2)])
        weight_left()
        ring_left()
        left(reduce_first() + reduce_second() + gather_z() + gather_minor())
        for ab in range(2):
            left(gather_major(ab) + [hand_over(ab, d) for d in range(majors[ab])])

    return kernel


def exchange(nx, ny, nz, dp, inter, dpre, keys, table, accum, scale):
    samples, width = dp.shape[3:]
    rows = accum.shape[1]
    pairs, hidden = inter.shape[1], dpre.shape[1]
    b = pairs // 4 // nz
    far = nz // 2
    nm = max(nx, ny)
    dma = pltpu.SemaphoreType.DMA
    vmem = pltpu.VMEM
    scratch = [
        vmem((2, 2, nm - 1, nm - 1, samples // 2, width), BF),
        vmem((2, 2, nx, ny, samples, width), BF),
        vmem((2,) + keys.shape, jnp.int32),
        vmem((2, rows, width), F32),
        vmem((2, 2, far, rows, width), BF),
        vmem((2, 2, far, rows, width), BF),
        vmem((2, nz, nm, nm, b, 128), BF),
        vmem((2, nz, nm, nm, b, 128), BF),
        vmem((2, nz, nm, nm, b, 128), F32),
        vmem((2, far, 2, nm, nm, b, 128), BF),
        vmem((2, far, 2, nm, nm, b, 128), BF),
        vmem((2, nm, nm, b, 128), F32),
        vmem((2, nm - 1, nm, b, 128), F32),
        vmem((2, nm, b, 128), F32),
        vmem((2, nm - 1, b, 128), F32),
        vmem((2, nz * b, 128), BF),
        dma((2,)),
        dma((2, 2, nm - 1, nm)), dma((2, 2, nm - 1, nm)),
        dma((2, 2, nm, nm - 1)), dma((2, 2, nm, nm - 1)),
        dma((2, 2)),
        dma((2, nx)), dma((2, nx)),
        dma((2, 2, far, 2)), dma((2, 2, far, 2)),
        dma((2,)), dma((2,)),
        dma((2, far, 2)), dma((2, far, 2)),
        dma((2, nm - 1)), dma((2, nm - 1)), dma((2, nm - 1)), dma((2, nm - 1)),
        dma((nz - 1,)), dma((nz - 1,)),
        dma((2, nm - 1)), dma((2, nm - 1)), dma((2, nm - 1)), dma((2, nm - 1)),
        dma((2, nm)), dma((2, nm)),
    ]
    in_vmem = pl.BlockSpec(memory_space=vmem)
    return pl.pallas_call(
        make_kernel(nx, ny, nz, samples, width, rows, scale),
        out_shape=(
            jax.ShapeDtypeStruct((pairs, hidden), BF),
            jax.ShapeDtypeStruct(table.shape, F32),
            jax.ShapeDtypeStruct(accum.shape, F32),
        ),
        in_specs=[in_vmem] * 6,
        out_specs=(in_vmem,) * 3,
        scratch_shapes=scratch,
        compiler_params=pltpu.CompilerParams(
            collective_id=0, has_side_effects=True, vmem_limit_bytes=40 << 20
        ),
        name="exchange",
    )(dp, inter, dpre, keys, table, accum)


def solution(mesh):
    nx = ny = math.isqrt(mesh.shape["group"])
    nz = mesh.shape["hash"] // 2
    fine = Mesh(mesh.devices.reshape(nx, ny, nz, 2), AXES)
    group, hashed = ("x", "y"), ("z", "core")

    def local(pooled, weight, cotangent, owners, local_rows, table, accum):
        vectors = pooled[0]
        samples, feats, width = vectors.shape
        rows = accum.shape[1]
        inter = jnp.einsum(
            "sfe,sge->sfg", vectors, vectors, preferred_element_type=F32
        ).astype(BF)
        inter_rows = inter.reshape(samples, feats * feats)
        preact = jnp.dot(inter_rows, weight, preferred_element_type=F32)
        sig = jax.nn.sigmoid(preact)
        dpre = (cotangent[0].astype(F32) * (sig * (1.0 + preact * (1.0 - sig)))).astype(BF)
        dinter = lax.dot_general(
            dpre, weight, (((1,), (1,)), ((), ())), preferred_element_type=F32
        ).reshape(samples, feats, feats)
        dsym = (dinter + jnp.swapaxes(dinter, 1, 2)).astype(BF)
        dpooled = jnp.einsum("sfg,sge->fse", dsym, vectors, preferred_element_type=F32).astype(BF)
        keys = owners[0] * rows + local_rows[0]
        keys = keys.reshape(2, nx, ny * samples, 2).transpose(1, 0, 3, 2).reshape(nx, 4, ny * samples)
        return exchange(
            nx, ny, nz, dpooled.reshape(nx, ny, 2, samples, width), inter_rows, dpre, keys, table, accum,
            1.0 / math.sqrt(samples * nx * ny * nz * 2),
        )

    return jax.shard_map(
        local,
        mesh=fine,
        in_specs=(
            P(hashed, group, None, None),
            P(),
            P(hashed, group, None),
            P(hashed, group, None, None),
            P(hashed, group, None, None),
            P(group, hashed, None),
            P(group, hashed),
        ),
        out_specs=(P(), P(group, hashed, None), P(group, hashed)),
        check_vma=False,
    )
```

```python
import math

import jax
import jax.numpy as jnp
from jax import lax
from jax.experimental import pallas as pl
from jax.experimental.pallas import tpu as pltpu
from jax.sharding import Mesh, PartitionSpec as P

AXES = ("x", "y", "z", "core")
BF = jnp.bfloat16
F32 = jnp.float32


def make_kernel(nx, ny, nz, samples, width, rows, scale):
    far = nz // 2
    half_s = samples // 2
    half_r = rows // 2
    majors = (nx, ny)
    minors = (ny, nx)

    def kernel(
        dp, inter, dpre, keys, table, accum, wout, tout, aout,
        a1, v, kbuf, tot, sb, rb, sw, rw, w, wsb, wrb, s, r1, t, r2, gz,
        ks, f1s, f1r, f2s, f2r, loc, vs, vr, zs, zr, ws, wr, wzs, wzr,
        x1s, x1r, x2s, x2r, g0s, g0r, g1s, g1r, g2s, g2r, hs, hr,
    ):
        x, y, z, c = (lax.axis_index(a) for a in AXES)
        here = {"x": (x, nx), "y": (y, ny), "z": (z, nz), "core": (c, 2)}
        other = 1 - c

        def peer(axis, d):
            me, n = here[axis]
            return lax.rem(me + d + n, n)

        def remote(src, dst, ssem, rsem, axis, d):
            place = {a: here[a][0] for a in AXES}
            place[axis] = peer(axis, d)
            return pltpu.make_async_remote_copy(
                src, dst, ssem, rsem,
                device_id=tuple(place[a] for a in AXES), device_id_type=pl.DeviceIdType.MESH,
            )

        def start(copies):
            for copy in copies:
                copy.start()

        def arrived(copies):
            for copy in copies:
                copy.wait_recv()

        def left(copies):
            for copy in copies:
                copy.wait_send()

        barrier = pltpu.get_barrier_semaphore()
        greeted = 0
        for axis, n in (("core", 2), ("x", nx), ("y", ny), ("z", nz)):
            for d in range(1, n):
                place = {a: here[a][0] for a in AXES}
                place[axis] = peer(axis, d)
                pl.semaphore_signal(
                    barrier, inc=1, device_id=tuple(place[a] for a in AXES),
                    device_id_type=pl.DeviceIdType.MESH,
                )
                greeted += 1

        firsts, seconds = ("x", "y"), ("y", "x")
        lead, trail = (x, y), (y, x)

        def piece(ab, p, q, j):
            p, q = (p, q) if ab == 0 else (q, p)
            return dp.at[p, q, j, pl.ds(ab * half_s, half_s), :]

        def place_of(ab, p, q, j):
            p, q = (p, q) if ab == 0 else (q, p)
            return v.at[j, c, p, q, pl.ds(ab * half_s, half_s), :]

        def hop_direct(j, ab):
            return [
                remote(
                    piece(ab, lead[ab], peer(seconds[ab], e), j), place_of(ab, lead[ab], trail[ab], j),
                    f2s.at[j, ab, 0, e - 1], f2r.at[j, ab, 0, e - 1], seconds[ab], e,
                )
                for e in range(1, minors[ab])
            ]

        def hop_first(j, ab, e):
            copies = []
            for d in range(1, majors[ab]):
                q = peer(seconds[ab], e)
                src = piece(ab, peer(firsts[ab], d), q, j)
                dst = place_of(ab, lead[ab], trail[ab], j) if e == 0 else a1.at[j, ab, d - 1, e - 1]
                copies.append(remote(
                    src, dst, f1s.at[j, ab, d - 1, e], f1r.at[j, ab, d - 1, e], firsts[ab], d,
                ))
            return copies

        def hop_second(j, ab, d, e):
            origin = peer(firsts[ab], -d)
            return remote(
                a1.at[j, ab, d - 1, e - 1], place_of(ab, origin, trail[ab], j),
                f2s.at[j, ab, d, e - 1], f2r.at[j, ab, d, e - 1], seconds[ab], e,
            )

        def own_pieces(j):
            return [
                pltpu.make_async_copy(
                    piece(ab, lead[ab], trail[ab], j), place_of(ab, lead[ab], trail[ab], j), loc.at[j, ab]
                )
                for ab in range(2)
            ]

        def hop_start(j):
            for e in range(1, max(nx, ny)):
                for ab in range(2):
                    if e < minors[ab]:
                        start(hop_first(j, ab, e))
            for ab in range(2):
                start(hop_direct(j, ab))
            for ab in range(2):
                start(hop_first(j, ab, 0))
            start(own_pieces(j))

        def hop_forward(j, distances=None):
            for e in distances or range(1, max(nx, ny)):
                for ab in range(2):
                    if e < minors[ab]:
                        for d, copy in enumerate(hop_first(j, ab, e), 1):
                            copy.wait_recv()
                            hop_second(j, ab, d, e).start()

        def share(j, d):
            p = peer("x", -d)
            return remote(v.at[j, c, p], v.at[j, c, p], vs.at[j, d], vr.at[j, d], "core", 1)

        def hop_end(j):
            for copy in own_pieces(j):
                copy.wait()
            for d in range(nx):
                if d == 0:
                    arrived(hop_direct(j, 0))
                    arrived(hop_first(j, 1, 0))
                else:
                    hop_first(j, 0, 0)[d - 1].wait_recv()
                    arrived([hop_second(j, 0, d, e) for e in range(1, ny)])
                    hop_direct(j, 1)[d - 1].wait_recv()
                    arrived([hop_second(j, 1, q, d) for q in range(1, ny)])
                share(j, d).start()

        def shared(j):
            arrived([share(j, d) for d in range(nx)])

        def hop_left(j):
            for ab in range(2):
                left(hop_direct(j, ab))
                for e in range(minors[ab]):
                    left(hop_first(j, ab, e))
                for d in range(1, majors[ab]):
                    left([hop_second(j, ab, d, e) for e in range(1, minors[ab])])
            left([share(j, d) for d in range(nx)])

        def key_copy():
            return remote(keys, kbuf.at[c], ks.at[0], ks.at[1], "core", 1)

        def term(core, ab, m):
            r = nz * w.shape[4]
            cols = minors[ab] * 128
            return lax.dot_general(
                inter[:, pl.ds(pl.multiple_of((core * 2 + ab) * r, 128), r)],
                dpre[:, m * cols : (m + 1) * cols],
                (((0,), (0,)), ((), ())),
                preferred_element_type=F32,
            )

        def term_into(ref, core, ab):
            b = w.shape[4]
            for m in range(majors[ab]):
                block = term(core, ab, m).astype(ref.dtype)
                for n in range(minors[ab]):
                    for q in range(nz):
                        ref[ab, q, m, n] = block[q * b : (q + 1) * b, n * 128 : (n + 1) * 128]

        def term_across():
            return [
                remote(sw.at[ab, q], rw.at[ab, q], ws.at[ab, q], wr.at[ab, q], "core", 1)
                for ab in range(2) for q in range(nz)
            ]

        def term_own():
            for ab in range(2):
                term_into(w, c, ab)


        def toward(way, k):
            return peer("z", k if way == 0 else -k)

        def comes(k, way, half):
            return k < far or (k == far and way == half)

        def weight_copy(k, way, half):
            return remote(
                wsb.at[way, k - 1, half], wrb.at[way, k - 1, half],
                wzs.at[way, k - 1, half], wzr.at[way, k - 1, half], "z", 1 if way == 0 else -1,
            )

        def weight_step(k):
            for way, half in ((0, 0), (1, 1), (0, 1), (1, 0)):
                if comes(k, way, half):
                    dest = toward(way, k)
                    total = w[half, dest] + rw[half, dest].astype(F32)
                    if comes(k + 1, way, half):
                        weight_copy(k + 1, way, half).wait_recv()
                        total = total + wrb[way, k, half].astype(F32)
                    wsb[way, k - 1, half] = total.astype(BF)
                    weight_copy(k, way, half).start()

        def weight_end():
            for half in range(2):
                total = w[half, z] + rw[half, z].astype(F32)
                for way in range(2):
                    if comes(1, way, half):
                        weight_copy(1, way, half).wait_recv()
                        total = total + wrb[way, 0, half].astype(F32)
                s[half] = total

        def weight_left():
            for k in range(1, far + 1):
                for way in range(2):
                    for half in range(2):
                        if comes(k, way, half):
                            weight_copy(k, way, half).wait_send()

        def reduce_first():
            return [
                remote(
                    s.at[ab, peer(firsts[ab], d)], r1.at[ab, d - 1],
                    x1s.at[ab, d - 1], x1r.at[ab, d - 1], firsts[ab], d,
                )
                for ab in range(2) for d in range(1, majors[ab])
            ]

        def sum_first():
            for ab in range(2):
                total = s[ab, lead[ab]]
                for d in range(majors[ab] - 1):
                    total = total + r1[ab, d]
                t[ab] = total

        def reduce_second():
            return [
                remote(
                    t.at[ab, peer(seconds[ab], d)], r2.at[ab, d - 1],
                    x2s.at[ab, d - 1], x2r.at[ab, d - 1], seconds[ab], d,
                )
                for ab in range(2) for d in range(1, minors[ab])
            ]

        piece_rows = w.shape[4]
        quarter = nz * piece_rows

        def my_rows():
            return pl.ds(pl.multiple_of(z * piece_rows, 16), piece_rows)

        def sum_second():
            for ab in range(2):
                total = t[ab, trail[ab]]
                for d in range(minors[ab] - 1):
                    total = total + r2[ab, d]
                gz[ab, my_rows(), :] = (total * scale).astype(BF)

        def gather_z():
            return [
                remote(
                    gz.at[:, my_rows(), :], gz.at[:, my_rows(), :], g0s.at[d - 1], g0r.at[d - 1], "z", d
                )
                for d in range(1, nz)
            ]

        def out_block(core, ab, m, n=None):
            r = pl.ds(pl.multiple_of((core * 2 + ab) * quarter, 16), quarter)
            if n is None:
                cols = pl.ds(pl.multiple_of(m * (minors[ab] * 128), 128), minors[ab] * 128)
            else:
                cols = pl.ds(pl.multiple_of((m * minors[ab] + n) * 128, 128), 128)
            return r, cols

        def gather_minor():
            copies = []
            for ab in range(2):
                r, cols = out_block(c, ab, lead[ab], trail[ab])
                copies += [
                    remote(gz.at[ab], wout.at[r, cols], g1s.at[ab, d - 1], g1r.at[ab, d - 1], seconds[ab], d)
                    for d in range(1, minors[ab])
                ]
            return copies

        def keep_minor():
            for ab in range(2):
                r, cols = out_block(c, ab, lead[ab], trail[ab])
                wout[r, cols] = gz[ab]

        def gather_major(ab):
            r, cols = out_block(c, ab, lead[ab])
            return [
                remote(wout.at[r, cols], wout.at[r, cols], g2s.at[ab, d - 1], g2r.at[ab, d - 1], firsts[ab], d)
                for d in range(1, majors[ab])
            ]

        def hand_over(ab, d):
            r, cols = out_block(c, ab, peer(firsts[ab], -d))
            return remote(wout.at[r, cols], wout.at[r, cols], hs.at[ab, d], hr.at[ab, d], "core", 1)

        def partial(j, dest, slot):
            base = (2 * dest + c) * rows
            iota = lax.broadcasted_iota(jnp.int32, (rows, ny * samples), 0).astype(jnp.int16)
            acc = None
            for q in range(2 * nx):
                h = c if q < nx else other
                i = q % nx
                first = (kbuf[h, i, pl.ds(2 * j, 1), :] - base).astype(jnp.int16)
                second = (kbuf[h, i, pl.ds(2 * j + 1, 1), :] - base).astype(jnp.int16)
                hot = jnp.where((iota == first) | (iota == second), BF(1), BF(0))
                prod = jnp.dot(
                    hot, v[j, h, i].reshape(ny * samples, width), preferred_element_type=F32
                )
                acc = prod if acc is None else acc + prod
            tot[slot] = acc

        def part(half):
            return pl.ds(half * half_r, half_r)

        def ring_copy(j, k, way, half):
            step = 1 - 2 * way
            return remote(
                sb.at[j, way, k - 1, part(half), :], rb.at[j, way, k - 1, part(half), :],
                zs.at[j, way, k - 1, half], zr.at[j, way, k - 1, half], "z", step,
            )

        def turn(step, between):
            early = step < far
            j = jnp.where(early | (step == far + 1), 0, 1)
            k = jnp.where(early, far - step, 2 * far + 1 - step)
            k = jnp.where(step == far, far, jnp.where(step == far + 1, 0, k))

            def one(way, carry):
                partial(j, peer("z", k * (1 - 2 * way)), way)
                return carry

            lax.fori_loop(0, jnp.where((k == 0) | (k == far), 1, 2), one, 0)

            @pl.when(k == far)
            def _():
                for half in range(2):
                    sb[j, half, far - 1, part(half), :] = tot[0, part(half), :].astype(BF)
                    ring_copy(j, far, half, half).start()

            if far > 1:
                @pl.when((k > 0) & (k < far))
                def _():
                    for way, half in ((0, 0), (1, 1)):
                        ring_copy(j, k + 1, way, half).wait_recv()
                        sb[j, way, k - 1, part(half), :] = (
                            tot[way, part(half), :] + rb[j, way, k, part(half), :].astype(F32)
                        ).astype(BF)
                        ring_copy(j, k, way, half).start()

                between()

                @pl.when(k == far - 1)
                def _():
                    for way, half in ((0, 1), (1, 0)):
                        sb[j, way, far - 2, part(half), :] = tot[way, part(half), :].astype(BF)
                        ring_copy(j, far - 1, way, half).start()

            if far > 2:
                @pl.when((k > 0) & (k < far - 1))
                def _():
                    for way, half in ((0, 1), (1, 0)):
                        ring_copy(j, k + 1, way, half).wait_recv()
                        sb[j, way, k - 1, part(half), :] = (
                            tot[way, part(half), :] + rb[j, way, k, part(half), :].astype(F32)
                        ).astype(BF)
                        ring_copy(j, k, way, half).start()

            @pl.when(k == 0)
            def _():
                for half in range(2):
                    for w_ in range(2):
                        if comes(1, w_, half):
                            ring_copy(j, 1, w_, half).wait_recv()
                rowgrad = tot[0]
                if far > 1:
                    rowgrad = rowgrad + rb[j, 0, 0].astype(F32) + rb[j, 1, 0].astype(F32)
                else:
                    rowgrad = rowgrad + jnp.concatenate(
                        [rb[j, 0, 0, part(0), :], rb[j, 1, 0, part(1), :]], axis=0
                    ).astype(F32)
                old = jnp.transpose(jnp.broadcast_to(accum[pl.ds(j, 1), :], (128, rows)))[:, 0:1]
                new = old + jnp.sum(rowgrad * rowgrad, axis=1, keepdims=True) * (1.0 / width)
                aout[pl.ds(j, 1), :] = jnp.transpose(jnp.broadcast_to(new, (rows, 128)))[0:1, :]
                tout[j] = table[j] - 0.1 * rowgrad / jnp.sqrt(new)

        def ring_left():
            for j in range(2):
                for k in range(1, far + 1):
                    for way in range(2):
                        for half in range(2):
                            if comes(k, way, half):
                                ring_copy(j, k, way, half).wait_send()

        def finish_second():
            arrived(reduce_second())
            sum_second()
            start(gather_z())

        def begin_reduce():
            weight_end()
            start(reduce_first())

        def middle_reduce():
            arrived(reduce_first())
            sum_first()
            start(reduce_second())

        def begin_gather():
            arrived(gather_z())
            start(gather_minor())
            keep_minor()

        def begin_major():
            arrived(gather_minor())
            for ab in range(2):
                start(gather_major(ab))
                hand_over(ab, 0).start()

        def hand_on(distances):
            for d in distances:
                for ab in range(2 if d < nx else 0):
                    gather_major(ab)[d - 1].wait_recv()
                    hand_over(ab, d).start()

        for ab in range(2):
            term_into(sw, other, ab)
        pl.semaphore_wait(barrier, greeted)
        hop_start(0)
        key_copy().start()
        kbuf[c] = keys[...]
        start(term_across())
        term_own()
        arrived(term_across())
        weight_step(far)
        hop_forward(0, (1,))
        weight_step(far - 1)
        hop_forward(0, (2, 3))
        weight_step(far - 2)
        hop_end(0)
        hop_start(1)
        key_copy().wait_recv()
        shared(0)

        midway = (
            (1, (lambda: begin_reduce(),)),
            (2, (lambda: finish_second(),)),
            (3, (lambda: begin_gather(),)),
        )
        after = (
            (0, (lambda: weight_step(1),)),
            (1, (lambda: hop_forward(1), lambda: middle_reduce(),)),
            (2, (lambda: hop_end(1),)),
            (3, (lambda: shared(1), lambda: begin_major(),)),
            (7, (lambda: hand_on((1, 3)),)),
            (8, (lambda: hand_on((2,)),)),
        )

        def run(tasks, step):
            for at, group in tasks:
                for task in group:
                    pl.when(step == at)(task)

        def body(step, carry):
            turn(step, lambda: run(midway, step))
            run(after, step)
            return carry

        lax.fori_loop(0, 2 * (far + 1), body, 0)

        for ab in range(2):
            for d in range(majors[ab]):
                hand_over(ab, d).wait_recv()
        for j in range(2):
            hop_left(j)
        left([key_copy()] + term_across())
        weight_left()
        ring_left()
        left(reduce_first() + reduce_second() + gather_z() + gather_minor())
        for ab in range(2):
            left(gather_major(ab) + [hand_over(ab, d) for d in range(majors[ab])])

    return kernel


def exchange(nx, ny, nz, dp, inter, dpre, keys, table, accum, scale):
    samples, width = dp.shape[3:]
    rows = accum.shape[1]
    pairs, hidden = inter.shape[1], dpre.shape[1]
    b = pairs // 4 // nz
    far = nz // 2
    nm = max(nx, ny)
    dma = pltpu.SemaphoreType.DMA
    vmem = pltpu.VMEM
    scratch = [
        vmem((2, 2, nm - 1, nm - 1, samples // 2, width), BF),
        vmem((2, 2, nx, ny, samples, width), BF),
        vmem((2,) + keys.shape, jnp.int32),
        vmem((2, rows, width), F32),
        vmem((2, 2, far, rows, width), BF),
        vmem((2, 2, far, rows, width), BF),
        vmem((2, nz, nm, nm, b, 128), BF),
        vmem((2, nz, nm, nm, b, 128), BF),
        vmem((2, nz, nm, nm, b, 128), F32),
        vmem((2, far, 2, nm, nm, b, 128), BF),
        vmem((2, far, 2, nm, nm, b, 128), BF),
        vmem((2, nm, nm, b, 128), F32),
        vmem((2, nm - 1, nm, b, 128), F32),
        vmem((2, nm, b, 128), F32),
        vmem((2, nm - 1, b, 128), F32),
        vmem((2, nz * b, 128), BF),
        dma((2,)),
        dma((2, 2, nm - 1, nm)), dma((2, 2, nm - 1, nm)),
        dma((2, 2, nm, nm - 1)), dma((2, 2, nm, nm - 1)),
        dma((2, 2)),
        dma((2, nx)), dma((2, nx)),
        dma((2, 2, far, 2)), dma((2, 2, far, 2)),
        dma((2, nz)), dma((2, nz)),
        dma((2, far, 2)), dma((2, far, 2)),
        dma((2, nm - 1)), dma((2, nm - 1)), dma((2, nm - 1)), dma((2, nm - 1)),
        dma((nz - 1,)), dma((nz - 1,)),
        dma((2, nm - 1)), dma((2, nm - 1)), dma((2, nm - 1)), dma((2, nm - 1)),
        dma((2, nm)), dma((2, nm)),
    ]
    in_vmem = pl.BlockSpec(memory_space=vmem)
    return pl.pallas_call(
        make_kernel(nx, ny, nz, samples, width, rows, scale),
        out_shape=(
            jax.ShapeDtypeStruct((pairs, hidden), BF),
            jax.ShapeDtypeStruct(table.shape, F32),
            jax.ShapeDtypeStruct(accum.shape, F32),
        ),
        in_specs=[in_vmem] * 6,
        out_specs=(in_vmem,) * 3,
        scratch_shapes=scratch,
        compiler_params=pltpu.CompilerParams(
            collective_id=0, has_side_effects=True, vmem_limit_bytes=40 << 20
        ),
        name="exchange",
    )(dp, inter, dpre, keys, table, accum)


def solution(mesh):
    nx = ny = math.isqrt(mesh.shape["group"])
    nz = mesh.shape["hash"] // 2
    fine = Mesh(mesh.devices.reshape(nx, ny, nz, 2), AXES)
    group, hashed = ("x", "y"), ("z", "core")

    def local(pooled, weight, cotangent, owners, local_rows, table, accum):
        vectors = pooled[0]
        samples, feats, width = vectors.shape
        rows = accum.shape[1]
        inter = jnp.einsum(
            "sfe,sge->sfg", vectors, vectors, preferred_element_type=F32
        ).astype(BF)
        inter_rows = inter.reshape(samples, feats * feats)
        preact = jnp.dot(inter_rows, weight, preferred_element_type=F32)
        sig = jax.nn.sigmoid(preact)
        dpre = (cotangent[0].astype(F32) * (sig * (1.0 + preact * (1.0 - sig)))).astype(BF)
        dinter = lax.dot_general(
            dpre, weight, (((1,), (1,)), ((), ())), preferred_element_type=F32
        ).reshape(samples, feats, feats)
        dsym = (dinter + jnp.swapaxes(dinter, 1, 2)).astype(BF)
        dpooled = jnp.einsum("sfg,sge->fse", dsym, vectors, preferred_element_type=F32).astype(BF)
        keys = owners[0] * rows + local_rows[0]
        keys = keys.reshape(2, nx, ny * samples, 2).transpose(1, 0, 3, 2).reshape(nx, 4, ny * samples)
        return exchange(
            nx, ny, nz, dpooled.reshape(nx, ny, 2, samples, width), inter_rows, dpre, keys, table, accum,
            1.0 / math.sqrt(samples * nx * ny * nz * 2),
        )

    return jax.shard_map(
        local,
        mesh=fine,
        in_specs=(
            P(hashed, group, None, None),
            P(),
            P(hashed, group, None),
            P(hashed, group, None, None),
            P(hashed, group, None, None),
            P(group, hashed, None),
            P(group, hashed),
        ),
        out_specs=(P(), P(group, hashed, None), P(group, hashed)),
        check_vma=False,
    )
```

```python
import math

import jax
import jax.numpy as jnp
from jax import lax
from jax.experimental import pallas as pl
from jax.experimental.pallas import tpu as pltpu
from jax.sharding import Mesh, PartitionSpec as P

AXES = ("x", "y", "z", "core")
BF = jnp.bfloat16
F32 = jnp.float32


def make_kernel(nx, ny, nz, samples, width, rows, scale):
    far = nz // 2
    half_s = samples // 2
    half_r = rows // 2
    majors = (nx, ny)
    minors = (ny, nx)

    def kernel(
        dp, inter, dpre, keys, table, accum, wout, tout, aout,
        a1, v, kbuf, tot, sb, rb, sw, rw, w, wsb, wrb, s, r1, t, r2, gz,
        ks, f1s, f1r, f2s, f2r, loc, vs, vr, zs, zr, ws, wr, wzs, wzr,
        x1s, x1r, x2s, x2r, g0s, g0r, g1s, g1r, g2s, g2r, hs, hr,
    ):
        x, y, z, c = (lax.axis_index(a) for a in AXES)
        here = {"x": (x, nx), "y": (y, ny), "z": (z, nz), "core": (c, 2)}
        other = 1 - c

        def peer(axis, d):
            me, n = here[axis]
            return lax.rem(me + d + n, n)

        def remote(src, dst, ssem, rsem, axis, d):
            place = {a: here[a][0] for a in AXES}
            place[axis] = peer(axis, d)
            return pltpu.make_async_remote_copy(
                src, dst, ssem, rsem,
                device_id=tuple(place[a] for a in AXES), device_id_type=pl.DeviceIdType.MESH,
            )

        def start(copies):
            for copy in copies:
                copy.start()

        def arrived(copies):
            for copy in copies:
                copy.wait_recv()

        def left(copies):
            for copy in copies:
                copy.wait_send()

        barrier = pltpu.get_barrier_semaphore()
        greeted = 0
        for axis, n in (("core", 2), ("x", nx), ("y", ny), ("z", nz)):
            for d in range(1, n):
                place = {a: here[a][0] for a in AXES}
                place[axis] = peer(axis, d)
                pl.semaphore_signal(
                    barrier, inc=1, device_id=tuple(place[a] for a in AXES),
                    device_id_type=pl.DeviceIdType.MESH,
                )
                greeted += 1
        pl.semaphore_wait(barrier, greeted)

        firsts, seconds = ("x", "y"), ("y", "x")
        lead, trail = (x, y), (y, x)

        def piece(ab, p, q, j):
            p, q = (p, q) if ab == 0 else (q, p)
            return dp.at[p, q, j, pl.ds(ab * half_s, half_s), :]

        def place_of(ab, p, q, j):
            p, q = (p, q) if ab == 0 else (q, p)
            return v.at[j, c, p, q, pl.ds(ab * half_s, half_s), :]

        def hop_direct(j, ab):
            return [
                remote(
                    piece(ab, lead[ab], peer(seconds[ab], e), j), place_of(ab, lead[ab], trail[ab], j),
                    f2s.at[j, ab, 0, e - 1], f2r.at[j, ab, 0, e - 1], seconds[ab], e,
                )
                for e in range(1, minors[ab])
            ]

        def hop_first(j, ab, e):
            copies = []
            for d in range(1, majors[ab]):
                q = peer(seconds[ab], e)
                src = piece(ab, peer(firsts[ab], d), q, j)
                dst = place_of(ab, lead[ab], trail[ab], j) if e == 0 else a1.at[j, ab, d - 1, e - 1]
                copies.append(remote(
                    src, dst, f1s.at[j, ab, d - 1, e], f1r.at[j, ab, d - 1, e], firsts[ab], d,
                ))
            return copies

        def hop_second(j, ab, d, e):
            origin = peer(firsts[ab], -d)
            return remote(
                a1.at[j, ab, d - 1, e - 1], place_of(ab, origin, trail[ab], j),
                f2s.at[j, ab, d, e - 1], f2r.at[j, ab, d, e - 1], seconds[ab], e,
            )

        def own_pieces(j):
            return [
                pltpu.make_async_copy(
                    piece(ab, lead[ab], trail[ab], j), place_of(ab, lead[ab], trail[ab], j), loc.at[j, ab]
                )
                for ab in range(2)
            ]

        def hop_start(j):
            for e in range(1, max(nx, ny)):
                for ab in range(2):
                    if e < minors[ab]:
                        start(hop_first(j, ab, e))
            for ab in range(2):
                start(hop_direct(j, ab))
            for ab in range(2):
                start(hop_first(j, ab, 0))
            start(own_pieces(j))

        def hop_forward(j):
            for e in range(1, max(nx, ny)):
                for ab in range(2):
                    if e < minors[ab]:
                        for d, copy in enumerate(hop_first(j, ab, e), 1):
                            copy.wait_recv()
                            hop_second(j, ab, d, e).start()

        def share(j, d):
            p = peer("x", -d)
            return remote(v.at[j, c, p], v.at[j, c, p], vs.at[j, d], vr.at[j, d], "core", 1)

        def hop_end(j):
            for copy in own_pieces(j):
                copy.wait()
            for d in range(nx):
                if d == 0:
                    arrived(hop_direct(j, 0))
                    arrived(hop_first(j, 1, 0))
                else:
                    hop_first(j, 0, 0)[d - 1].wait_recv()
                    arrived([hop_second(j, 0, d, e) for e in range(1, ny)])
                    hop_direct(j, 1)[d - 1].wait_recv()
                    arrived([hop_second(j, 1, q, d) for q in range(1, ny)])
                share(j, d).start()

        def shared(j):
            arrived([share(j, d) for d in range(nx)])

        def hop_left(j):
            for ab in range(2):
                left(hop_direct(j, ab))
                for e in range(minors[ab]):
                    left(hop_first(j, ab, e))
                for d in range(1, majors[ab]):
                    left([hop_second(j, ab, d, e) for e in range(1, minors[ab])])
            left([share(j, d) for d in range(nx)])

        def key_copy():
            return remote(keys, kbuf.at[c], ks.at[0], ks.at[1], "core", 1)

        def term(core, ab, m):
            r = nz * w.shape[4]
            cols = minors[ab] * 128
            return lax.dot_general(
                inter[:, pl.ds(pl.multiple_of((core * 2 + ab) * r, 128), r)],
                dpre[:, m * cols : (m + 1) * cols],
                (((0,), (0,)), ((), ())),
                preferred_element_type=F32,
            )

        def term_into(ref, core, ab):
            b = w.shape[4]
            for m in range(majors[ab]):
                block = term(core, ab, m).astype(ref.dtype)
                for n in range(minors[ab]):
                    for q in range(nz):
                        ref[ab, q, m, n] = block[q * b : (q + 1) * b, n * 128 : (n + 1) * 128]

        def term_across(ab):
            return remote(sw.at[ab], rw.at[ab], ws.at[ab], wr.at[ab], "core", 1)

        def toward(way, k):
            return peer("z", k if way == 0 else -k)

        def comes(k, way, half):
            return k < far or (k == far and way == half)

        def weight_copy(k, way, half):
            return remote(
                wsb.at[way, k - 1, half], wrb.at[way, k - 1, half],
                wzs.at[way, k - 1, half], wzr.at[way, k - 1, half], "z", 1 if way == 0 else -1,
            )

        def weight_step(k):
            for way, half in ((0, 0), (1, 1), (0, 1), (1, 0)):
                if comes(k, way, half):
                    dest = toward(way, k)
                    total = w[half, dest] + rw[half, dest].astype(F32)
                    if comes(k + 1, way, half):
                        weight_copy(k + 1, way, half).wait_recv()
                        total = total + wrb[way, k, half].astype(F32)
                    wsb[way, k - 1, half] = total.astype(BF)
                    weight_copy(k, way, half).start()

        def weight_end():
            for half in range(2):
                total = w[half, z] + rw[half, z].astype(F32)
                for way in range(2):
                    if comes(1, way, half):
                        weight_copy(1, way, half).wait_recv()
                        total = total + wrb[way, 0, half].astype(F32)
                s[half] = total

        def weight_left():
            for k in range(1, far + 1):
                for way in range(2):
                    for half in range(2):
                        if comes(k, way, half):
                            weight_copy(k, way, half).wait_send()

        def reduce_first():
            return [
                remote(
                    s.at[ab, peer(firsts[ab], d)], r1.at[ab, d - 1],
                    x1s.at[ab, d - 1], x1r.at[ab, d - 1], firsts[ab], d,
                )
                for ab in range(2) for d in range(1, majors[ab])
            ]

        def sum_first():
            for ab in range(2):
                total = s[ab, lead[ab]]
                for d in range(majors[ab] - 1):
                    total = total + r1[ab, d]
                t[ab] = total

        def reduce_second():
            return [
                remote(
                    t.at[ab, peer(seconds[ab], d)], r2.at[ab, d - 1],
                    x2s.at[ab, d - 1], x2r.at[ab, d - 1], seconds[ab], d,
                )
                for ab in range(2) for d in range(1, minors[ab])
            ]

        piece_rows = w.shape[4]
        quarter = nz * piece_rows

        def my_rows():
            return pl.ds(pl.multiple_of(z * piece_rows, 16), piece_rows)

        def sum_second():
            for ab in range(2):
                total = t[ab, trail[ab]]
                for d in range(minors[ab] - 1):
                    total = total + r2[ab, d]
                gz[ab, my_rows(), :] = (total * scale).astype(BF)

        def gather_z():
            return [
                remote(
                    gz.at[:, my_rows(), :], gz.at[:, my_rows(), :], g0s.at[d - 1], g0r.at[d - 1], "z", d
                )
                for d in range(1, nz)
            ]

        def out_block(core, ab, m, n=None):
            r = pl.ds(pl.multiple_of((core * 2 + ab) * quarter, 16), quarter)
            if n is None:
                cols = pl.ds(pl.multiple_of(m * (minors[ab] * 128), 128), minors[ab] * 128)
            else:
                cols = pl.ds(pl.multiple_of((m * minors[ab] + n) * 128, 128), 128)
            return r, cols

        def gather_minor():
            copies = []
            for ab in range(2):
                r, cols = out_block(c, ab, lead[ab], trail[ab])
                copies += [
                    remote(gz.at[ab], wout.at[r, cols], g1s.at[ab, d - 1], g1r.at[ab, d - 1], seconds[ab], d)
                    for d in range(1, minors[ab])
                ]
            return copies

        def keep_minor():
            for ab in range(2):
                r, cols = out_block(c, ab, lead[ab], trail[ab])
                wout[r, cols] = gz[ab]

        def gather_major(ab):
            r, cols = out_block(c, ab, lead[ab])
            return [
                remote(wout.at[r, cols], wout.at[r, cols], g2s.at[ab, d - 1], g2r.at[ab, d - 1], firsts[ab], d)
                for d in range(1, majors[ab])
            ]

        def hand_over(ab, d):
            r, cols = out_block(c, ab, peer(firsts[ab], -d))
            return remote(wout.at[r, cols], wout.at[r, cols], hs.at[ab, d], hr.at[ab, d], "core", 1)

        def partial(j, dest, slot):
            base = (2 * dest + c) * rows
            iota = lax.broadcasted_iota(jnp.int32, (rows, ny * samples), 0).astype(jnp.int16)
            acc = None
            for q in range(2 * nx):
                h = c if q < nx else other
                i = q % nx
                first = (kbuf[h, i, pl.ds(2 * j, 1), :] - base).astype(jnp.int16)
                second = (kbuf[h, i, pl.ds(2 * j + 1, 1), :] - base).astype(jnp.int16)
                hot = jnp.where((iota == first) | (iota == second), BF(1), BF(0))
                prod = jnp.dot(
                    hot, v[j, h, i].reshape(ny * samples, width), preferred_element_type=F32
                )
                acc = prod if acc is None else acc + prod
            tot[slot] = acc

        def part(half):
            return pl.ds(half * half_r, half_r)

        def ring_copy(j, k, way, half):
            step = 1 - 2 * way
            return remote(
                sb.at[j, way, k - 1, part(half), :], rb.at[j, way, k - 1, part(half), :],
                zs.at[j, way, k - 1, half], zr.at[j, way, k - 1, half], "z", step,
            )

        def turn(step):
            early = step < far
            j = jnp.where(early | (step == far + 1), 0, 1)
            k = jnp.where(early, far - step, 2 * far + 1 - step)
            k = jnp.where(step == far, far, jnp.where(step == far + 1, 0, k))

            def one(way, carry):
                partial(j, peer("z", k * (1 - 2 * way)), way)
                return carry

            lax.fori_loop(0, jnp.where((k == 0) | (k == far), 1, 2), one, 0)

            @pl.when(k == far)
            def _():
                for half in range(2):
                    sb[j, half, far - 1, part(half), :] = tot[0, part(half), :].astype(BF)
                    ring_copy(j, far, half, half).start()

            if far > 1:
                @pl.when((k > 0) & (k < far))
                def _():
                    for way, half in ((0, 0), (1, 1)):
                        ring_copy(j, k + 1, way, half).wait_recv()
                        sb[j, way, k - 1, part(half), :] = (
                            tot[way, part(half), :] + rb[j, way, k, part(half), :].astype(F32)
                        ).astype(BF)
                        ring_copy(j, k, way, half).start()

                @pl.when(k == far - 1)
                def _():
                    for way, half in ((0, 1), (1, 0)):
                        sb[j, way, far - 2, part(half), :] = tot[way, part(half), :].astype(BF)
                        ring_copy(j, far - 1, way, half).start()

            if far > 2:
                @pl.when((k > 0) & (k < far - 1))
                def _():
                    for way, half in ((0, 1), (1, 0)):
                        ring_copy(j, k + 1, way, half).wait_recv()
                        sb[j, way, k - 1, part(half), :] = (
                            tot[way, part(half), :] + rb[j, way, k, part(half), :].astype(F32)
                        ).astype(BF)
                        ring_copy(j, k, way, half).start()

            @pl.when(k == 0)
            def _():
                for half in range(2):
                    for w_ in range(2):
                        if comes(1, w_, half):
                            ring_copy(j, 1, w_, half).wait_recv()
                rowgrad = tot[0]
                if far > 1:
                    rowgrad = rowgrad + rb[j, 0, 0].astype(F32) + rb[j, 1, 0].astype(F32)
                else:
                    rowgrad = rowgrad + jnp.concatenate(
                        [rb[j, 0, 0, part(0), :], rb[j, 1, 0, part(1), :]], axis=0
                    ).astype(F32)
                old = jnp.transpose(jnp.broadcast_to(accum[pl.ds(j, 1), :], (128, rows)))[:, 0:1]
                new = old + jnp.sum(rowgrad * rowgrad, axis=1, keepdims=True) * (1.0 / width)
                aout[pl.ds(j, 1), :] = jnp.transpose(jnp.broadcast_to(new, (rows, 128)))[0:1, :]
                tout[j] = table[j] - 0.1 * rowgrad / jnp.sqrt(new)

        def ring_left():
            for j in range(2):
                for k in range(1, far + 1):
                    for way in range(2):
                        for half in range(2):
                            if comes(k, way, half):
                                ring_copy(j, k, way, half).wait_send()

        hop_start(0)
        key_copy().start()
        kbuf[c] = keys[...]
        for ab in range(2):
            term_into(sw, other, ab)
            term_across(ab).start()
        for ab in range(2):
            term_into(w, c, ab)
        arrived([term_across(ab) for ab in range(2)])
        weight_step(far)
        hop_forward(0)
        if far > 1:
            weight_step(far - 1)
        hop_end(0)
        hop_start(1)
        key_copy().wait_recv()
        shared(0)

        def late_steps(last):
            for k in range(far - 2, 0, -1):
                if (k == 1) == last:
                    weight_step(k)

        def finish_second():
            arrived(reduce_second())
            sum_second()
            start(gather_z())

        def begin_reduce():
            weight_end()
            start(reduce_first())

        def middle_reduce():
            arrived(reduce_first())
            sum_first()
            start(reduce_second())

        def begin_gather():
            arrived(gather_z())
            start(gather_minor())
            keep_minor()

        def begin_major():
            arrived(gather_minor())
            for ab in range(2):
                start(gather_major(ab))
                hand_over(ab, 0).start()

        def hand_on():
            for d in sorted(range(1, nx), key=lambda d: min(d, nx - d)):
                for ab in range(2):
                    gather_major(ab)[d - 1].wait_recv()
                    hand_over(ab, d).start()

        tasks = (
            [lambda: late_steps(False)],
            [lambda: late_steps(True), lambda: hop_forward(1)],
            [begin_reduce],
            [lambda: hop_end(1), middle_reduce, lambda: shared(1)],
            [finish_second],
            [begin_gather],
            [begin_major],
            [],
            [hand_on],
        )

        def body(step, carry):
            turn(step)
            for at, group in enumerate(tasks):
                for task in group:
                    pl.when(step == (min(at, far - 1) if at < 4 else min(at - 4 + far, 2 * far + 1)))(task)
            return carry

        lax.fori_loop(0, 2 * (far + 1), body, 0)

        for ab in range(2):
            for d in range(majors[ab]):
                hand_over(ab, d).wait_recv()
        for j in range(2):
            hop_left(j)
        left([key_copy()] + [term_across(ab) for ab in range(2)])
        weight_left()
        ring_left()
        left(reduce_first() + reduce_second() + gather_z() + gather_minor())
        for ab in range(2):
            left(gather_major(ab) + [hand_over(ab, d) for d in range(majors[ab])])

    return kernel


def exchange(nx, ny, nz, dp, inter, dpre, keys, table, accum, scale):
    samples, width = dp.shape[3:]
    rows = accum.shape[1]
    pairs, hidden = inter.shape[1], dpre.shape[1]
    b = pairs // 4 // nz
    far = nz // 2
    nm = max(nx, ny)
    dma = pltpu.SemaphoreType.DMA
    vmem = pltpu.VMEM
    scratch = [
        vmem((2, 2, nm - 1, nm - 1, samples // 2, width), BF),
        vmem((2, 2, nx, ny, samples, width), BF),
        vmem((2,) + keys.shape, jnp.int32),
        vmem((2, rows, width), F32),
        vmem((2, 2, far, rows, width), BF),
        vmem((2, 2, far, rows, width), BF),
        vmem((2, nz, nm, nm, b, 128), BF),
        vmem((2, nz, nm, nm, b, 128), BF),
        vmem((2, nz, nm, nm, b, 128), F32),
        vmem((2, far, 2, nm, nm, b, 128), BF),
        vmem((2, far, 2, nm, nm, b, 128), BF),
        vmem((2, nm, nm, b, 128), F32),
        vmem((2, nm - 1, nm, b, 128), F32),
        vmem((2, nm, b, 128), F32),
        vmem((2, nm - 1, b, 128), F32),
        vmem((2, nz * b, 128), BF),
        dma((2,)),
        dma((2, 2, nm - 1, nm)), dma((2, 2, nm - 1, nm)),
        dma((2, 2, nm, nm - 1)), dma((2, 2, nm, nm - 1)),
        dma((2, 2)),
        dma((2, nx)), dma((2, nx)),
        dma((2, 2, far, 2)), dma((2, 2, far, 2)),
        dma((2,)), dma((2,)),
        dma((2, far, 2)), dma((2, far, 2)),
        dma((2, nm - 1)), dma((2, nm - 1)), dma((2, nm - 1)), dma((2, nm - 1)),
        dma((nz - 1,)), dma((nz - 1,)),
        dma((2, nm - 1)), dma((2, nm - 1)), dma((2, nm - 1)), dma((2, nm - 1)),
        dma((2, nm)), dma((2, nm)),
    ]
    in_vmem = pl.BlockSpec(memory_space=vmem)
    return pl.pallas_call(
        make_kernel(nx, ny, nz, samples, width, rows, scale),
        out_shape=(
            jax.ShapeDtypeStruct((pairs, hidden), BF),
            jax.ShapeDtypeStruct(table.shape, F32),
            jax.ShapeDtypeStruct(accum.shape, F32),
        ),
        in_specs=[in_vmem] * 6,
        out_specs=(in_vmem,) * 3,
        scratch_shapes=scratch,
        compiler_params=pltpu.CompilerParams(
            collective_id=0, has_side_effects=True, vmem_limit_bytes=40 << 20
        ),
        name="exchange",
    )(dp, inter, dpre, keys, table, accum)


def solution(mesh):
    nx = ny = math.isqrt(mesh.shape["group"])
    nz = mesh.shape["hash"] // 2
    fine = Mesh(mesh.devices.reshape(nx, ny, nz, 2), AXES)
    group, hashed = ("x", "y"), ("z", "core")

    def local(pooled, weight, cotangent, owners, local_rows, table, accum):
        vectors = pooled[0]
        samples, feats, width = vectors.shape
        rows = accum.shape[1]
        inter = jnp.einsum(
            "sfe,sge->sfg", vectors, vectors, preferred_element_type=F32
        ).astype(BF)
        inter_rows = inter.reshape(samples, feats * feats)
        preact = jnp.dot(inter_rows, weight, preferred_element_type=F32)
        sig = jax.nn.sigmoid(preact)
        dpre = (cotangent[0].astype(F32) * (sig * (1.0 + preact * (1.0 - sig)))).astype(BF)
        dinter = lax.dot_general(
            dpre, weight, (((1,), (1,)), ((), ())), preferred_element_type=F32
        ).reshape(samples, feats, feats)
        dsym = (dinter + jnp.swapaxes(dinter, 1, 2)).astype(BF)
        dpooled = jnp.einsum("sfg,sge->fse", dsym, vectors, preferred_element_type=F32).astype(BF)
        keys = owners[0] * rows + local_rows[0]
        keys = keys.reshape(2, nx, ny * samples, 2).transpose(1, 0, 3, 2).reshape(nx, 4, ny * samples)
        return exchange(
            nx, ny, nz, dpooled.reshape(nx, ny, 2, samples, width), inter_rows, dpre, keys, table, accum,
            1.0 / math.sqrt(samples * nx * ny * nz * 2),
        )

    return jax.shard_map(
        local,
        mesh=fine,
        in_specs=(
            P(hashed, group, None, None),
            P(),
            P(hashed, group, None),
            P(hashed, group, None, None),
            P(hashed, group, None, None),
            P(group, hashed, None),
            P(group, hashed),
        ),
        out_specs=(P(), P(group, hashed, None), P(group, hashed)),
        check_vma=False,
    )
```
